256 devices in a mesh: xy: 8 (over y, x_lo), zt: 32 (over z, x_hi, core).
Axes of the slice: x: 4 (x_hi: 2, x_lo: 2; x = x_hi * 2 + x_lo), y: 4, z: 8, core: 2. Of those that a mesh axis runs over, the one named last changes fastest.
Arguments:
- links: float32 [4, 18, 64, 128, 384], P(None, None, 'xy', 'zt'), may hold values from -3.4 to 3.4
- solution: float32 [6, 64, 128, 384], P(None, 'xy', 'zt'), may hold values from -6 to 6
- product: float32 [6, 64, 128, 384], P(None, 'xy', 'zt'), may hold values from -6 to 6
Outputs:
- force: float32 [4, 18, 64, 128, 384], P(None, None, 'xy', 'zt')
The draws below stay inside these ranges and needn't reach their ends.
All inputs are finite; a program needn't handle non-finite values.
Results may differ from the reference program's by a relative error of at most 0.00002.
Values sent between devices are 32-bit elements; how exact they have to be, the bound alone decides.
No kernel may reach another device: no remote copies, remote signals or barrier semaphores. Data moves between devices by JAX's collectives and lax.ppermute only.
A program may use at most 64 MiB of HBM per device.

```python
import jax
import jax.numpy as jnp

NT = 24
NX = 64
NZ = 128
YT = 384


def level_of(own_key, extent, split, smallest, largest):
    level, own = 1.0, jax.random.fold_in(own_key, 6)
    for axis_at, parts in split:
        steps = jnp.exp(jax.random.uniform(jax.random.fold_in(own, axis_at), (parts,), jnp.float32, smallest / len(split), largest / len(split)))
        level = level * jnp.repeat(steps, extent[axis_at] // parts).reshape([-1 if axis == axis_at else 1 for axis in range(len(extent))])
    return level


def gaussian(key, shape, scale, reach, pieces=(), kind=jnp.bfloat16):
    result = jax.random.normal(key, shape, jnp.float32) * scale
    if len(pieces) > 0:
        result = level_of(key, shape, pieces, -0.22, 0.18) * result
    return jnp.clip(result, min=-reach, max=reach).astype(kind)


def setup_inputs(seed: int = 0) -> dict:
    key_list = jax.random.split(jax.random.key(seed), 4)
    links = gaussian(key_list[0], (4, 18, NX, NZ, YT), 0.577, 3.4, ((2, 8), (3, 32)), jnp.float32)
    solution = gaussian(key_list[1], (6, NX, NZ, YT), 1.0, 6.0, ((1, 8), (2, 32)), jnp.float32)
    product = gaussian(key_list[2], (6, NX, NZ, YT), 1.0, 6.0, ((1, 8), (2, 32)), jnp.float32)
    return {"links": links, "solution": solution, "product": product}


coef_one = 9.0 / 8.0
coef_naik = -1.0 / 24.0


def link_parts(link):
    rest = link.shape[1:]
    return link[:9].reshape((3, 3) + rest), link[9:].reshape((3, 3) + rest)


def apply_link(link, vector):
    real_u, imag_u = link_parts(link)
    real_v, imag_v = vector[:3], vector[3:]
    real_out = jnp.sum(real_u * real_v[None], axis=1) - jnp.sum(imag_u * imag_v[None], axis=1)
    imag_out = jnp.sum(real_u * imag_v[None], axis=1) + jnp.sum(imag_u * real_v[None], axis=1)
    return jnp.concatenate([real_out, imag_out], axis=0)


def apply_adjoint(link, vector):
    real_u, imag_u = link_parts(link)
    real_v, imag_v = vector[:3], vector[3:]
    real_out = jnp.sum(real_u * real_v[:, None] + imag_u * imag_v[:, None], axis=0)
    imag_out = jnp.sum(real_u * imag_v[:, None] - imag_u * real_v[:, None], axis=0)
    return jnp.concatenate([real_out, imag_out], axis=0)


def outer_conj(left, right):
    real_l, imag_l = left[:3], left[3:]
    real_r, imag_r = right[:3], right[3:]
    rest = left.shape[1:]
    real_out = real_l[:, None] * real_r[None] + imag_l[:, None] * imag_r[None]
    imag_out = imag_l[:, None] * real_r[None] - real_l[:, None] * imag_r[None]
    return jnp.concatenate([real_out.reshape((9,) + rest), imag_out.reshape((9,) + rest)], axis=0)


def assemble(ahead_x, here_y, ahead_p2, ahead_p1, back_q1, back_q2):
    naik = outer_conj(ahead_p2, here_y) + outer_conj(ahead_p1, back_q1) + outer_conj(ahead_x, back_q2)
    return coef_one * outer_conj(ahead_x, here_y) + coef_naik * naik


def force_dir(link, solution, product, mover):
    ahead_x = mover(solution, 1)
    first = apply_link(link, ahead_x)
    ahead_p1 = mover(first, 1)
    second = apply_link(link, ahead_p1)
    ahead_p2 = mover(second, 1)
    back_q1 = mover(apply_adjoint(link, product), -1)
    back_q2 = mover(apply_adjoint(link, back_q1), -1)
    return assemble(ahead_x, product, ahead_p2, ahead_p1, back_q1, back_q2)


def move_time(field, step, slices):
    width = field.shape[-1]
    tpos = jnp.arange(width, dtype=jnp.int32) % slices
    if step > 0:
        return jnp.where(tpos < slices - step, jnp.roll(field, -step, axis=-1), jnp.roll(field, slices - step, axis=-1))
    return jnp.where(tpos >= -step, jnp.roll(field, -step, axis=-1), jnp.roll(field, -step - slices, axis=-1))


def reference(links, solution, product):
    def move_x(field, step):
        return jnp.roll(field, -step, axis=1)

    def move_y(field, step):
        return jnp.roll(field, -step * NT, axis=3)

    def move_z(field, step):
        return jnp.roll(field, -step, axis=2)

    def move_t(field, step):
        return move_time(field, step, NT)

    movers = [move_x, move_y, move_z, move_t]
    forces = [force_dir(links[m], solution, product, movers[m]) for m in range(4)]
    return jnp.stack(forces, axis=0)
```

```python
import jax
import jax.numpy as jnp
from jax import lax
from jax.experimental import pallas as pl
from jax.experimental.pallas import tpu as pltpu
from jax.sharding import PartitionSpec as P

NT = 24
CX, CZ, YT, YB = 8, 4, 384, 3
ROWS = YB * CX * CZ

coef_one = 9.0 / 8.0
coef_naik = -1.0 / 24.0

F32 = jnp.float32


def mat_vec(u, v):
    out_r, out_i = [], []
    for a in range(3):
        re = im = None
        for b in range(3):
            ur, ui = u(3 * a + b), u(9 + 3 * a + b)
            r = ur * v[b] - ui * v[3 + b]
            i = ur * v[3 + b] + ui * v[b]
            re, im = (r, i) if re is None else (re + r, im + i)
        out_r.append(re)
        out_i.append(im)
    return out_r + out_i


def adj_vec(u, v):
    out_r, out_i = [], []
    for a in range(3):
        re = im = None
        for b in range(3):
            ur, ui = u(3 * b + a), u(9 + 3 * b + a)
            r = ur * v[b] + ui * v[3 + b]
            i = ur * v[3 + b] - ui * v[b]
            re, im = (r, i) if re is None else (re + r, im + i)
        out_r.append(re)
        out_i.append(im)
    return out_r + out_i


def store_force(put, v1, y, p1, q1, x, q2):
    for a in range(3):
        for b in range(3):
            re = im = None
            for p, q in ((v1, y), (p1, q1), (x, q2)):
                r = p[a] * q[b] + p[3 + a] * q[3 + b]
                i = p[3 + a] * q[b] - p[a] * q[3 + b]
                re, im = (r, i) if re is None else (re + r, im + i)
            put(3 * a + b, re)
            put(9 + 3 * a + b, im)


def tiles(ref):
    return ref.reshape(ref.shape[0], YB, CX, CZ, 128)


def lanes(yb):
    return pl.ds(128 * yb, 128)


def prep_kernel(links, sol, prod, zf, zb, xf, xb, ul, xs, ys, sem):
    copies = []

    def load(src, dst):
        copy = pltpu.make_async_copy(src, dst, sem.at[len(copies)])
        copy.start()
        copies.append(copy)

    ult, xst, yst = tiles(ul), tiles(xs), tiles(ys)
    for yb in range(YB):
        load(links.at[2, :, :, :, lanes(yb)], ult.at[pl.ds(18, 18), yb])
        load(sol.at[:, :, :, lanes(yb)], xst.at[:, yb])
        load(prod.at[:, :, :, lanes(yb)], yst.at[:, yb])
    for yb in range(YB):
        load(links.at[0, :, :, :, lanes(yb)], ult.at[pl.ds(0, 18), yb])
    for copy in copies[:9]:
        copy.wait()

    def layer(z):
        return pl.ds(z, YB * CX, stride=CZ)

    def uz(z):
        return lambda c: ul[18 + c, layer(z), :]

    def vec(ref, rows):
        return [ref[c, rows, :] for c in range(6)]

    p1_0 = mat_vec(uz(0), vec(xs, layer(1)))
    p2_0 = mat_vec(uz(0), mat_vec(uz(1), vec(xs, layer(2))))
    for c, value in enumerate(vec(xs, layer(0)) + p1_0 + p2_0):
        zf[c] = value
    q1 = [coef_naik * v for v in adj_vec(uz(3), vec(ys, layer(3)))]
    q2 = adj_vec(uz(3), [coef_naik * v for v in adj_vec(uz(2), vec(ys, layer(2)))])
    for c, value in enumerate(q1 + q2):
        zb[c] = value
    for copy in copies[9:]:
        copy.wait()
    for yb in range(YB):
        base = yb * CX * CZ

        def ux(row):
            return lambda c: ul[c, pl.ds(row, 8), :]

        p1 = mat_vec(ux(base), vec(xs, pl.ds(base + CZ, 8)))
        p2 = mat_vec(ux(base), [pltpu.roll(v, 4, 0) for v in p1])
        for c, value in enumerate(vec(xs, pl.ds(base, 8)) + p1 + p2):
            xf[c, yb] = value[:CZ]
        last = base + (CX - 2) * CZ
        w1 = [coef_naik * v for v in adj_vec(ux(last), vec(ys, pl.ds(last, 8)))]
        w2 = adj_vec(ux(last), [pltpu.roll(v, 4, 0) for v in w1])
        for c, value in enumerate(w1 + w2):
            xb[c, yb] = value[CZ:]


def move_y(v, step):
    lane = lax.broadcasted_iota(jnp.int32, (8, 128), 1)
    if step > 0:
        r = [pltpu.roll(a, 128 - NT, 1) for a in v]
        return [jnp.where(lane < 128 - NT, r[k], r[(k + 1) % YB]) for k in range(YB)]
    r = [pltpu.roll(a, NT, 1) for a in v]
    return [jnp.where(lane >= NT, r[k], r[(k - 1) % YB]) for k in range(YB)]


def move_t(v, step):
    lane = lax.broadcasted_iota(jnp.int32, (8, 128), 1)
    out = []
    if step > 0:
        near = [pltpu.roll(a, 127, 1) for a in v]
        wrap = [pltpu.roll(a, NT - 1, 1) for a in v]
        for k in range(YB):
            edge = (lane + 128 * k) % NT == NT - 1
            far = wrap[k] if k == 0 else jnp.where(lane < NT - 1, wrap[k - 1], wrap[k])
            beside = near[k] if k == YB - 1 else jnp.where(lane == 127, near[k + 1], near[k])
            out.append(jnp.where(edge, far, beside))
        return out
    near = [pltpu.roll(a, 1, 1) for a in v]
    wrap = [pltpu.roll(a, 128 - (NT - 1), 1) for a in v]
    for k in range(YB):
        edge = (lane + 128 * k) % NT == 0
        far = wrap[k] if k == YB - 1 else jnp.where(lane >= 128 - (NT - 1), wrap[k + 1], wrap[k])
        beside = near[k] if k == 0 else jnp.where(lane == 0, near[k - 1], near[k])
        out.append(jnp.where(edge, far, beside))
    return out


def local_kernel(links, xs, ys, force, ul, fs, sem_in, sem_out):
    ult, fst = tiles(ul), tiles(fs)
    loads = []
    for d, mu in enumerate((1, 3)):
        for yb in range(YB):
            copy = pltpu.make_async_copy(
                links.at[mu, :, :, :, lanes(yb)],
                ult.at[pl.ds(18 * d, 18), yb],
                sem_in.at[d * YB + yb],
            )
            copy.start()
            loads.append(copy)

    def out_copy(d, mu, yb, xp):
        return pltpu.make_async_copy(
            fst.at[pl.ds(18 * d, 18), yb, pl.ds(2 * xp, 2)],
            force.at[mu, :, pl.ds(2 * xp, 2), :, lanes(yb)],
            sem_out.at[(d * YB + yb) * 4 + xp],
        )

    for d, (mu, move) in enumerate(((1, move_y), (3, move_t))):
        for copy in loads[d * YB : (d + 1) * YB]:
            copy.wait()

        def body(xp, carry):
            rows = [pl.ds(pl.multiple_of(yb * CX * CZ + xp * 8, 8), 8) for yb in range(YB)]

            def shift(vecs, step):
                moved = [move([vecs[k][c] for k in range(YB)], step) for c in range(6)]
                return [[moved[c][k] for c in range(6)] for k in range(YB)]

            def u(k):
                return lambda c: ul[18 * d + c, rows[k], :]

            def vec(ref):
                return [[ref[c, rows[k], :] for c in range(6)] for k in range(YB)]

            x = shift(vec(xs), 1)
            p1 = shift([mat_vec(u(k), x[k]) for k in range(YB)], 1)
            p2 = shift([mat_vec(u(k), p1[k]) for k in range(YB)], 1)
            v1 = [[coef_one * a + coef_naik * b for a, b in zip(x[k], p2[k])] for k in range(YB)]
            y = vec(ys)
            q1 = [adj_vec(u(k), y[k]) for k in range(YB)]
            q1 = shift([[coef_naik * a for a in v] for v in q1], -1)
            q2 = shift([adj_vec(u(k), q1[k]) for k in range(YB)], -1)
            for k in range(YB):

                def put(c, value, k=k):
                    fs[18 * d + c, rows[k], :] = value

                store_force(put, v1[k], y[k], p1[k], q1[k], x[k], q2[k])
            for yb in range(YB):
                out_copy(d, mu, yb, xp).start()
            return carry

        lax.fori_loop(0, 4, body, 0)
    for d, mu in enumerate((1, 3)):
        for yb in range(YB):
            for xp in range(4):
                out_copy(d, mu, yb, xp).wait()


def edge_kernel(zf, zb, xf, xb, ul, xs, ys, _, force, fs, hz, hx, sem_out):
    fst = tiles(fs)
    row = lax.broadcasted_iota(jnp.int32, (8, 128), 0)

    for c in range(18):
        hz[c, pl.ds(CZ - 1, YB * CX, stride=CZ), :] = zf[c]
    for c in range(12):
        hz[c, pl.ds(0, YB * CX, stride=CZ), :] = zb[c]

    def out_z(yb):
        return pltpu.make_async_copy(
            fst.at[pl.ds(18, 18), yb], force.at[2, :, :, :, lanes(yb)], sem_out.at[yb]
        )

    def out_x(yb):
        return pltpu.make_async_copy(
            fst.at[pl.ds(0, 18), yb], force.at[0, :, :, :, lanes(yb)], sem_out.at[YB + yb]
        )

    def body_z(xp, yb):
        rows = pl.ds(pl.multiple_of(yb * CX * CZ + xp * 8, 8), 8)
        top, bottom = row % CZ == CZ - 1, row % CZ == 0

        def vec(ref, first=0):
            return [ref[first + c, rows, :] for c in range(6)]

        def ahead(v, first):
            return [jnp.where(top, h, pltpu.roll(a, 7, 0)) for a, h in zip(v, vec(hz, first))]

        def back(v, first):
            return [jnp.where(bottom, h, pltpu.roll(a, 1, 0)) for a, h in zip(v, vec(hz, first))]

        def u(c):
            return ul[18 + c, rows, :]

        x = ahead(vec(xs), 0)
        p1 = ahead(mat_vec(u, x), 6)
        p2 = ahead(mat_vec(u, p1), 12)
        v1 = [coef_one * a + coef_naik * b for a, b in zip(x, p2)]
        y = vec(ys)
        q1 = back([coef_naik * a for a in adj_vec(u, y)], 0)
        q2 = back(adj_vec(u, q1), 6)

        def put(c, value):
            fs[18 + c, rows, :] = value

        store_force(put, v1, y, p1, q1, x, q2)
        return yb

    for yb in range(YB):
        lax.fori_loop(0, 4, body_z, yb)
        out_z(yb).start()

    for yb in range(YB):
        for c in range(18):
            hx[c, pl.ds(yb * 8 + CZ, CZ), :] = xf[c, yb]
        for c in range(12):
            hx[c, pl.ds(yb * 8, CZ), :] = xb[c, yb]

    def body_x(yb, carry):
        rows = [pl.ds(pl.multiple_of(yb * CX * CZ + k * 8, 8), 8) for k in range(4)]
        edge = pl.ds(pl.multiple_of(yb * 8, 8), 8)
        low = row < CZ

        def vec(ref):
            return [[ref[c, rows[k], :] for c in range(6)] for k in range(4)]

        def half(vecs):
            return [[pltpu.roll(a, CZ, 0) for a in v] for v in vecs]

        def ahead(vecs, first):
            r = half(vecs) + [[hx[first + c, edge, :] for c in range(6)]]
            return [[jnp.where(low, a, b) for a, b in zip(r[k], r[k + 1])] for k in range(4)]

        def back(vecs, first):
            r = [[hx[first + c, edge, :] for c in range(6)]] + half(vecs)
            return [[jnp.where(low, a, b) for a, b in zip(r[k], r[k + 1])] for k in range(4)]

        def u(k):
            return lambda c: ul[c, rows[k], :]

        x = ahead(vec(xs), 0)
        p1 = ahead([mat_vec(u(k), x[k]) for k in range(4)], 6)
        p2 = ahead([mat_vec(u(k), p1[k]) for k in range(4)], 12)
        v1 = [[coef_one * a + coef_naik * b for a, b in zip(x[k], p2[k])] for k in range(4)]
        y = vec(ys)
        q1 = back([[coef_naik * a for a in adj_vec(u(k), y[k])] for k in range(4)], 0)
        q2 = back([adj_vec(u(k), q1[k]) for k in range(4)], 6)
        for k in range(4):

            def put(c, value, k=k):
                fs[c, rows[k], :] = value

            store_force(put, v1[k], y[k], p1[k], q1[k], x[k], q2[k])
        out_x(yb).start()
        return carry

    lax.fori_loop(0, YB, body_x, 0)
    for yb in range(YB):
        out_z(yb).wait()
        out_x(yb).wait()


HBM = pl.BlockSpec(memory_space=pltpu.HBM)
VM = pl.BlockSpec(memory_space=pltpu.VMEM)
MIB = 1 << 20


def per_device(links, solution, product):
    links, solution, product = (
        pltpu.with_memory_space_constraint(a, pltpu.HBM) for a in (links, solution, product)
    )
    zf, zb, xf, xb, ul, xs, ys = pl.pallas_call(
        prep_kernel,
        out_shape=(
            pltpu.VMEM((18, YB * CX, 128), F32),
            pltpu.VMEM((12, YB * CX, 128), F32),
            pltpu.VMEM((18, YB, CZ, 128), F32),
            pltpu.VMEM((12, YB, CZ, 128), F32),
            pltpu.VMEM((36, ROWS, 128), F32),
            pltpu.VMEM((6, ROWS, 128), F32),
            pltpu.VMEM((6, ROWS, 128), F32),
        ),
        in_specs=[HBM] * 3,
        out_specs=[VM] * 7,
        scratch_shapes=[pltpu.SemaphoreType.DMA((12,))],
        cost_estimate=pl.CostEstimate(flops=4000000, bytes_accessed=5000000, transcendentals=0),
        compiler_params=pltpu.CompilerParams(vmem_limit_bytes=16 * MIB),
        name="prep",
    )(links, solution, product)

    def ring(axis):
        size = lax.axis_size(axis)
        up = [(i, (i + 1) % size) for i in range(size)]
        return up, [(j, i) for i, j in up]

    up_z, down_z = ring("zt")
    up_x, down_x = ring("xy")
    zf = lax.ppermute(zf, "zt", down_z)
    zb = lax.ppermute(zb, "zt", up_z)
    xf = lax.ppermute(xf, "xy", down_x)
    xb = lax.ppermute(xb, "xy", up_x)

    force_shape = jax.ShapeDtypeStruct((4, 18, CX, CZ, YT), F32)
    force = pl.pallas_call(
        local_kernel,
        out_shape=force_shape,
        in_specs=[HBM, VM, VM],
        out_specs=HBM,
        scratch_shapes=[
            pltpu.VMEM((36, ROWS, 128), F32),
            pltpu.VMEM((36, ROWS, 128), F32),
            pltpu.SemaphoreType.DMA((6,)),
            pltpu.SemaphoreType.DMA((24,)),
        ],
        cost_estimate=pl.CostEstimate(flops=12000000, bytes_accessed=12000000, transcendentals=0),
        compiler_params=pltpu.CompilerParams(vmem_limit_bytes=16 * MIB),
        name="local",
    )(links, xs, ys)
    return pl.pallas_call(
        edge_kernel,
        out_shape=force_shape,
        in_specs=[VM] * 7 + [HBM],
        out_specs=HBM,
        input_output_aliases={7: 0},
        scratch_shapes=[
            pltpu.VMEM((36, ROWS, 128), F32),
            pltpu.VMEM((18, ROWS, 128), F32),
            pltpu.VMEM((18, YB * 8, 128), F32),
            pltpu.SemaphoreType.DMA((6,)),
        ],
        cost_estimate=pl.CostEstimate(flops=12000000, bytes_accessed=12000000, transcendentals=0),
        compiler_params=pltpu.CompilerParams(vmem_limit_bytes=16 * MIB),
        name="edge",
    )(zf, zb, xf, xb, ul, xs, ys, force)


def solution(mesh):
    placed = (P(None, None, "xy", "zt", None), P(None, "xy", "zt", None), P(None, "xy", "zt", None))
    return jax.shard_map(
        per_device,
        mesh=mesh,
        in_specs=placed,
        out_specs=P(None, None, "xy", "zt", None),
        check_vma=False,
    )
```

```python
import jax
import jax.numpy as jnp
from jax import lax
from jax.experimental import pallas as pl
from jax.experimental.pallas import tpu as pltpu
from jax.sharding import PartitionSpec as P

NT = 24
CX, CZ, YT, YB = 8, 4, 384, 3
ROWS = YB * CX * CZ

coef_one = 9.0 / 8.0
coef_naik = -1.0 / 24.0

F32 = jnp.float32


def mat_vec(u, v):
    out_r, out_i = [], []
    for a in range(3):
        re = im = None
        for b in range(3):
            ur, ui = u(3 * a + b), u(9 + 3 * a + b)
            r = ur * v[b] - ui * v[3 + b]
            i = ur * v[3 + b] + ui * v[b]
            re, im = (r, i) if re is None else (re + r, im + i)
        out_r.append(re)
        out_i.append(im)
    return out_r + out_i


def adj_vec(u, v):
    out_r, out_i = [], []
    for a in range(3):
        re = im = None
        for b in range(3):
            ur, ui = u(3 * b + a), u(9 + 3 * b + a)
            r = ur * v[b] + ui * v[3 + b]
            i = ur * v[3 + b] - ui * v[b]
            re, im = (r, i) if re is None else (re + r, im + i)
        out_r.append(re)
        out_i.append(im)
    return out_r + out_i


def store_force(put, v1, y, p1, q1, x, q2):
    for a in range(3):
        for b in range(3):
            re = im = None
            for p, q in ((v1, y), (p1, q1), (x, q2)):
                r = p[a] * q[b] + p[3 + a] * q[3 + b]
                i = p[3 + a] * q[b] - p[a] * q[3 + b]
                re, im = (r, i) if re is None else (re + r, im + i)
            put(3 * a + b, re)
            put(9 + 3 * a + b, im)


def tiles(ref):
    return ref.reshape(ref.shape[0], YB, CX, CZ, 128)


def lanes(yb):
    return pl.ds(128 * yb, 128)


class Loads:
    def __init__(self, sem):
        self.sem, self.copies, self.count = sem, {}, 0

    def start(self, name, src, dst):
        copy = pltpu.make_async_copy(src, dst, self.sem.at[self.count])
        copy.start()
        self.copies.setdefault(name, []).append(copy)
        self.count += 1

    def wait(self, name):
        for copy in self.copies.pop(name):
            copy.wait()


def vector(ref, rows, first=0):
    return [ref[first + c, rows, :] for c in range(6)]


def prep_kernel(links, sol, prod, xf, xb, ux, xs, ys, sem):
    loads = Loads(sem)
    uxt, xst, yst = tiles(ux), tiles(xs), tiles(ys)

    def load_x(name, first, count):
        for yb in range(YB):
            loads.start(
                name,
                links.at[0, :, pl.ds(first, count), :, lanes(yb)],
                uxt.at[:, yb, pl.ds(first, count)],
            )

    for yb in range(YB):
        loads.start("y", prod.at[:, :, :, lanes(yb)], yst.at[:, yb])
    load_x("last", CX - 2, 2)
    for yb in range(YB):
        loads.start("x", sol.at[:, :, :, lanes(yb)], xst.at[:, yb])
    load_x("first", 0, 2)
    load_x("inner", 2, CX - 4)

    def u(row):
        return lambda c: ux[c, pl.ds(row, 8), :]

    loads.wait("y")
    loads.wait("last")
    for yb in range(YB):
        last = yb * CX * CZ + (CX - 2) * CZ
        w1 = [coef_naik * v for v in adj_vec(u(last), vector(ys, pl.ds(last, 8)))]
        w2 = adj_vec(u(last), [pltpu.roll(v, 4, 0) for v in w1])
        for c, value in enumerate(w1 + w2):
            xb[c, yb] = value[CZ:]
    loads.wait("x")
    loads.wait("first")
    for yb in range(YB):
        base = yb * CX * CZ
        p1 = mat_vec(u(base), vector(xs, pl.ds(base + CZ, 8)))
        p2 = mat_vec(u(base), [pltpu.roll(v, 4, 0) for v in p1])
        for c, value in enumerate(vector(xs, pl.ds(base, 8)) + p1 + p2):
            xf[c, yb] = value[:CZ]
    loads.wait("inner")


def move_y(v, step):
    lane = lax.broadcasted_iota(jnp.int32, (8, 128), 1)
    if step > 0:
        r = [pltpu.roll(a, 128 - NT, 1) for a in v]
        return [jnp.where(lane < 128 - NT, r[k], r[(k + 1) % YB]) for k in range(YB)]
    r = [pltpu.roll(a, NT, 1) for a in v]
    return [jnp.where(lane >= NT, r[k], r[(k - 1) % YB]) for k in range(YB)]


def move_t(v, step):
    lane = lax.broadcasted_iota(jnp.int32, (8, 128), 1)
    out = []
    if step > 0:
        near = [pltpu.roll(a, 127, 1) for a in v]
        wrap = [pltpu.roll(a, NT - 1, 1) for a in v]
        for k in range(YB):
            edge = (lane + 128 * k) % NT == NT - 1
            far = wrap[k] if k == 0 else jnp.where(lane < NT - 1, wrap[k - 1], wrap[k])
            beside = near[k] if k == YB - 1 else jnp.where(lane == 127, near[k + 1], near[k])
            out.append(jnp.where(edge, far, beside))
        return out
    near = [pltpu.roll(a, 1, 1) for a in v]
    wrap = [pltpu.roll(a, 128 - (NT - 1), 1) for a in v]
    for k in range(YB):
        edge = (lane + 128 * k) % NT == 0
        far = wrap[k] if k == YB - 1 else jnp.where(lane >= 128 - (NT - 1), wrap[k + 1], wrap[k])
        beside = near[k] if k == 0 else jnp.where(lane == 0, near[k - 1], near[k])
        out.append(jnp.where(edge, far, beside))
    return out


def share():
    at = lax.axis_index("zt")
    return jnp.where(at == 0, 8, jnp.where(at == lax.axis_size("zt") - 1, 0, 4))


def local_piece(d, piece, move, ul, xs, ys, fs):
    rows = [pl.ds(pl.multiple_of(yb * CX * CZ + piece * 8, 8), 8) for yb in range(YB)]

    def shift(vecs, step):
        moved = [move([vecs[k][c] for k in range(YB)], step) for c in range(6)]
        return [[moved[c][k] for c in range(6)] for k in range(YB)]

    def u(k):
        return lambda c: ul[18 * (d + 1) + c, rows[k], :]

    x = shift([vector(xs, r) for r in rows], 1)
    p1 = shift([mat_vec(u(k), x[k]) for k in range(YB)], 1)
    p2 = shift([mat_vec(u(k), p1[k]) for k in range(YB)], 1)
    v1 = [[coef_one * a + coef_naik * b for a, b in zip(x[k], p2[k])] for k in range(YB)]
    y = [vector(ys, r) for r in rows]
    q1 = [adj_vec(u(k), y[k]) for k in range(YB)]
    q1 = shift([[coef_naik * a for a in v] for v in q1], -1)
    q2 = shift([adj_vec(u(k), q1[k]) for k in range(YB)], -1)
    for k in range(YB):

        def put(c, value, k=k):
            fs[18 * d + c, rows[k], :] = value

        store_force(put, v1[k], y[k], p1[k], q1[k], x[k], q2[k])


def early_kernel(links, xs, ys, zf, zb, ul, fs, sem):
    loads = Loads(sem)
    ult = tiles(ul)
    for d, mu in enumerate((2, 1, 3)):
        for yb in range(YB):
            loads.start(mu, links.at[mu, :, :, :, lanes(yb)], ult.at[pl.ds(18 * d, 18), yb])

    def layer(z):
        return pl.ds(z, YB * CX, stride=CZ)

    def u(z):
        return lambda c: ul[c, layer(z), :]

    loads.wait(2)
    q1 = [coef_naik * v for v in adj_vec(u(3), vector(ys, layer(3)))]
    q2 = adj_vec(u(3), [coef_naik * v for v in adj_vec(u(2), vector(ys, layer(2)))])
    for c, value in enumerate(q1 + q2):
        zb[c] = value
    p1 = mat_vec(u(0), vector(xs, layer(1)))
    p2 = mat_vec(u(0), mat_vec(u(1), vector(xs, layer(2))))
    for c, value in enumerate(vector(xs, layer(0)) + p1 + p2):
        zf[c] = value

    count = share()
    for d, (mu, move) in enumerate(((1, move_y), (3, move_t))):
        loads.wait(mu)

        def body(piece, carry):
            local_piece(d, piece, move, ul, xs, ys, fs)
            return carry

        lax.fori_loop(0, jnp.clip(count - 4 * d, 0, 4), body, 0)


def late_kernel(ul, xs, ys, done, force, fs, sem):
    count = share()

    def out_copy(src, d, piece, yb):
        return pltpu.make_async_copy(
            tiles(src).at[pl.ds(18 * d, 18), yb, pl.ds(2 * piece, 2)],
            force.at[2 * d + 1, :, pl.ds(2 * piece, 2), :, lanes(yb)],
            sem.at[(d * YB + yb) * 4 + piece],
        )

    for d, move in enumerate((move_y, move_t)):
        split = jnp.clip(count - 4 * d, 0, 4)

        def send(piece, carry):
            for yb in range(YB):
                out_copy(done, d, piece, yb).start()
            return carry

        def body(piece, carry):
            local_piece(d, piece, move, ul, xs, ys, fs)
            for yb in range(YB):
                out_copy(fs, d, piece, yb).start()
            return carry

        lax.fori_loop(0, split, send, 0)
        lax.fori_loop(split, 4, body, 0)
    for d in range(2):
        for yb in range(YB):
            for piece in range(4):
                out_copy(fs, d, piece, yb).wait()


def edge_x_kernel(xf, xb, ux, xs, ys, fx, hx):
    low = lax.broadcasted_iota(jnp.int32, (8, 128), 0) < CZ
    for yb in range(YB):
        for c in range(18):
            hx[c, pl.ds(yb * 8 + CZ, CZ), :] = xf[c, yb]
        for c in range(12):
            hx[c, pl.ds(yb * 8, CZ), :] = xb[c, yb]

    def body(yb, carry):
        rows = [pl.ds(pl.multiple_of(yb * CX * CZ + k * 8, 8), 8) for k in range(4)]
        edge = pl.ds(pl.multiple_of(yb * 8, 8), 8)

        def half(vecs):
            return [[pltpu.roll(a, CZ, 0) for a in v] for v in vecs]

        def joined(r):
            return [[jnp.where(low, a, b) for a, b in zip(r[k], r[k + 1])] for k in range(4)]

        def ahead(vecs, first):
            return joined(half(vecs) + [vector(hx, edge, first)])

        def back(vecs, first):
            return joined([vector(hx, edge, first)] + half(vecs))

        def u(k):
            return lambda c: ux[c, rows[k], :]

        x = ahead([vector(xs, r) for r in rows], 0)
        p1 = ahead([mat_vec(u(k), x[k]) for k in range(4)], 6)
        p2 = ahead([mat_vec(u(k), p1[k]) for k in range(4)], 12)
        v1 = [[coef_one * a + coef_naik * b for a, b in zip(x[k], p2[k])] for k in range(4)]
        y = [vector(ys, r) for r in rows]
        q1 = back([[coef_naik * a for a in adj_vec(u(k), y[k])] for k in range(4)], 0)
        q2 = back([adj_vec(u(k), q1[k]) for k in range(4)], 6)
        for k in range(4):

            def put(c, value, k=k):
                fx[c, rows[k], :] = value

            store_force(put, v1[k], y[k], p1[k], q1[k], x[k], q2[k])
        return carry

    lax.fori_loop(0, YB, body, 0)


def edge_z_kernel(zf, zb, ul, xs, ys, fx, _, force, fz, hz, sem):
    def out_copy(src, mu, yb):
        return pltpu.make_async_copy(
            tiles(src).at[:, yb], force.at[mu, :, :, :, lanes(yb)], sem.at[mu + yb * 4]
        )

    for yb in range(YB):
        out_copy(fx, 0, yb).start()
    for c in range(18):
        hz[c, pl.ds(CZ - 1, YB * CX, stride=CZ), :] = zf[c]
    for c in range(12):
        hz[c, pl.ds(0, YB * CX, stride=CZ), :] = zb[c]
    row = lax.broadcasted_iota(jnp.int32, (8, 128), 0)
    top, bottom = row % CZ == CZ - 1, row % CZ == 0

    def body(piece, yb):
        rows = pl.ds(pl.multiple_of(yb * CX * CZ + piece * 8, 8), 8)

        def ahead(v, first):
            halo = vector(hz, rows, first)
            return [jnp.where(top, h, pltpu.roll(a, 7, 0)) for a, h in zip(v, halo)]

        def back(v, first):
            halo = vector(hz, rows, first)
            return [jnp.where(bottom, h, pltpu.roll(a, 1, 0)) for a, h in zip(v, halo)]

        def u(c):
            return ul[c, rows, :]

        x = ahead(vector(xs, rows), 0)
        p1 = ahead(mat_vec(u, x), 6)
        p2 = ahead(mat_vec(u, p1), 12)
        v1 = [coef_one * a + coef_naik * b for a, b in zip(x, p2)]
        y = vector(ys, rows)
        q1 = back([coef_naik * a for a in adj_vec(u, y)], 0)
        q2 = back(adj_vec(u, q1), 6)

        def put(c, value):
            fz[c, rows, :] = value

        store_force(put, v1, y, p1, q1, x, q2)
        return yb

    for yb in range(YB):
        lax.fori_loop(0, 4, body, yb)
        out_copy(fz, 2, yb).start()
    for yb in range(YB):
        out_copy(fx, 0, yb).wait()
        out_copy(fz, 2, yb).wait()


HBM = pl.BlockSpec(memory_space=pltpu.HBM)
VM = pl.BlockSpec(memory_space=pltpu.VMEM)
FORCE = jax.ShapeDtypeStruct((4, 18, CX, CZ, YT), F32)


def held(*shape):
    return pltpu.VMEM(shape, F32)


def kernel_call(body, name, flops, **args):
    return pl.pallas_call(
        body,
        name=name,
        cost_estimate=pl.CostEstimate(flops=flops, bytes_accessed=flops, transcendentals=0),
        compiler_params=pltpu.CompilerParams(vmem_limit_bytes=16 << 20),
        **args,
    )


def shifted(value, axis, step):
    size = lax.axis_size(axis)
    return lax.ppermute(value, axis, [(i, (i + step) % size) for i in range(size)])


def per_device(links, solution, product):
    links, solution, product = (
        pltpu.with_memory_space_constraint(a, pltpu.HBM) for a in (links, solution, product)
    )
    dma = pltpu.SemaphoreType.DMA
    xf, xb, ux, xs, ys = kernel_call(
        prep_kernel,
        "prep",
        3000000,
        out_shape=(
            held(18, YB, CZ, 128),
            held(12, YB, CZ, 128),
            held(18, ROWS, 128),
            held(6, ROWS, 128),
            held(6, ROWS, 128),
        ),
        in_specs=[HBM] * 3,
        out_specs=[VM] * 5,
        scratch_shapes=[dma((15,))],
    )(links, solution, product)
    xb = shifted(xb, "xy", 1)
    xf = shifted(xf, "xy", -1)
    zf, zb, ul, done = kernel_call(
        early_kernel,
        "early",
        8000000,
        out_shape=(
            held(18, YB * CX, 128),
            held(12, YB * CX, 128),
            held(54, ROWS, 128),
            held(36, ROWS, 128),
        ),
        in_specs=[HBM, VM, VM],
        out_specs=[VM] * 4,
        scratch_shapes=[dma((9,))],
    )(links, xs, ys)
    zb = shifted(zb, "zt", 1)
    zf = shifted(zf, "zt", -1)
    force = kernel_call(
        late_kernel,
        "late",
        8000000,
        out_shape=FORCE,
        in_specs=[VM] * 4,
        out_specs=HBM,
        scratch_shapes=[held(36, ROWS, 128), dma((24,))],
    )(ul, xs, ys, done)
    fx = kernel_call(
        edge_x_kernel,
        "edge_x",
        4000000,
        out_shape=held(18, ROWS, 128),
        in_specs=[VM] * 5,
        out_specs=VM,
        scratch_shapes=[held(18, YB * 8, 128)],
    )(xf, xb, ux, xs, ys)
    return kernel_call(
        edge_z_kernel,
        "edge_z",
        4000000,
        out_shape=FORCE,
        in_specs=[VM] * 6 + [HBM],
        out_specs=HBM,
        input_output_aliases={6: 0},
        scratch_shapes=[held(18, ROWS, 128), held(18, ROWS, 128), dma((12,))],
    )(zf, zb, ul, xs, ys, fx, force)


def solution(mesh):
    placed = (P(None, None, "xy", "zt", None), P(None, "xy", "zt", None), P(None, "xy", "zt", None))
    return jax.shard_map(
        per_device,
        mesh=mesh,
        in_specs=placed,
        out_specs=P(None, None, "xy", "zt", None),
        check_vma=False,
    )
```

```python
import jax
import jax.numpy as jnp
from jax import lax
from jax.experimental import pallas as pl
from jax.experimental.pallas import tpu as pltpu
from jax.sharding import PartitionSpec as P

NT = 24
CX, CZ, YT, YB = 8, 4, 384, 3
ROWS = YB * CX * CZ

coef_one = 9.0 / 8.0
coef_naik = -1.0 / 24.0

F32 = jnp.float32

LOCAL_COST = 1200000000
EDGE_Z_COST = 4000000


def mat_vec(u, v):
    out_r, out_i = [], []
    for a in range(3):
        re = im = None
        for b in range(3):
            ur, ui = u(3 * a + b), u(9 + 3 * a + b)
            r = ur * v[b] - ui * v[3 + b]
            i = ur * v[3 + b] + ui * v[b]
            re, im = (r, i) if re is None else (re + r, im + i)
        out_r.append(re)
        out_i.append(im)
    return out_r + out_i


def adj_vec(u, v):
    out_r, out_i = [], []
    for a in range(3):
        re = im = None
        for b in range(3):
            ur, ui = u(3 * b + a), u(9 + 3 * b + a)
            r = ur * v[b] + ui * v[3 + b]
            i = ur * v[3 + b] - ui * v[b]
            re, im = (r, i) if re is None else (re + r, im + i)
        out_r.append(re)
        out_i.append(im)
    return out_r + out_i


def store_force(put, v1, y, p1, q1, x, q2):
    for a in range(3):
        for b in range(3):
            re = im = None
            for p, q in ((v1, y), (p1, q1), (x, q2)):
                r = p[a] * q[b] + p[3 + a] * q[3 + b]
                i = p[3 + a] * q[b] - p[a] * q[3 + b]
                re, im = (r, i) if re is None else (re + r, im + i)
            put(3 * a + b, re)
            put(9 + 3 * a + b, im)


def tiles(ref):
    return ref.reshape(ref.shape[0], YB, CX, CZ, 128)


def lanes(yb):
    return pl.ds(128 * yb, 128)


class Loads:
    def __init__(self, sem):
        self.sem, self.copies, self.count = sem, {}, 0

    def start(self, name, src, dst):
        copy = pltpu.make_async_copy(src, dst, self.sem.at[self.count])
        copy.start()
        self.copies.setdefault(name, []).append(copy)
        self.count += 1

    def wait(self, name):
        for copy in self.copies.pop(name):
            copy.wait()


def vector(ref, rows, first=0):
    return [ref[first + c, rows, :] for c in range(6)]


def prep_kernel(links, sol, prod, far, near, ux, uz, xs, ys, sem):
    loads = Loads(sem)
    uxt, uzt, xst, yst = tiles(ux), tiles(uz), tiles(xs), tiles(ys)
    for yb in range(YB):
        loads.start("x", sol.at[:, :, :, lanes(yb)], xst.at[:, yb])
    for yb in range(YB):
        loads.start("uz", links.at[2, :, :, :, lanes(yb)], uzt.at[:, yb])
    for yb in range(YB):
        loads.start("y", prod.at[:, :, :, lanes(yb)], yst.at[:, yb])
    for yb in range(YB):
        loads.start("ux", links.at[0, :, :, :, lanes(yb)], uxt.at[:, yb])

    def layer(z):
        return pl.ds(z, YB * CX, stride=CZ)

    def u_z(z):
        return lambda c: uz[c, layer(z), :]

    loads.wait("x")
    loads.wait("uz")
    p1 = mat_vec(u_z(0), vector(xs, layer(1)))
    p2 = mat_vec(u_z(0), mat_vec(u_z(1), vector(xs, layer(2))))
    ahead = vector(xs, layer(0)) + p1 + p2
    loads.wait("y")
    q1 = [coef_naik * v for v in adj_vec(u_z(3), vector(ys, layer(3)))]
    q2 = adj_vec(u_z(3), [coef_naik * v for v in adj_vec(u_z(2), vector(ys, layer(2)))])
    behind = q1 + q2

    def put(to_before, to_after):
        for c, value in enumerate(ahead):
            to_before[c] = value
        for c, value in enumerate(behind):
            to_after[c] = value

    odd = lax.axis_index("zt") % 2
    pl.when(odd == 0)(lambda: put(far, near))
    pl.when(odd == 1)(lambda: put(near, far))
    loads.wait("ux")


def move_y(v, step):
    lane = lax.broadcasted_iota(jnp.int32, (8, 128), 1)
    if step > 0:
        r = [pltpu.roll(a, 128 - NT, 1) for a in v]
        return [jnp.where(lane < 128 - NT, r[k], r[(k + 1) % YB]) for k in range(YB)]
    r = [pltpu.roll(a, NT, 1) for a in v]
    return [jnp.where(lane >= NT, r[k], r[(k - 1) % YB]) for k in range(YB)]


def move_t(v, step):
    lane = lax.broadcasted_iota(jnp.int32, (8, 128), 1)
    out = []
    if step > 0:
        near = [pltpu.roll(a, 127, 1) for a in v]
        wrap = [pltpu.roll(a, NT - 1, 1) for a in v]
        for k in range(YB):
            edge = (lane + 128 * k) % NT == NT - 1
            far = wrap[k] if k == 0 else jnp.where(lane < NT - 1, wrap[k - 1], wrap[k])
            beside = near[k] if k == YB - 1 else jnp.where(lane == 127, near[k + 1], near[k])
            out.append(jnp.where(edge, far, beside))
        return out
    near = [pltpu.roll(a, 1, 1) for a in v]
    wrap = [pltpu.roll(a, 128 - (NT - 1), 1) for a in v]
    for k in range(YB):
        edge = (lane + 128 * k) % NT == 0
        far = wrap[k] if k == YB - 1 else jnp.where(lane >= 128 - (NT - 1), wrap[k + 1], wrap[k])
        beside = near[k] if k == 0 else jnp.where(lane == 0, near[k - 1], near[k])
        out.append(jnp.where(edge, far, beside))
    return out


def local_piece(d, piece, move, ul, xs, ys, fs):
    rows = [pl.ds(pl.multiple_of(yb * CX * CZ + piece * 8, 8), 8) for yb in range(YB)]

    def shift(vecs, step):
        moved = [move([vecs[k][c] for k in range(YB)], step) for c in range(6)]
        return [[moved[c][k] for c in range(6)] for k in range(YB)]

    def u(k):
        return lambda c: ul[18 * d + c, rows[k], :]

    x = shift([vector(xs, r) for r in rows], 1)
    p1 = shift([mat_vec(u(k), x[k]) for k in range(YB)], 1)
    p2 = shift([mat_vec(u(k), p1[k]) for k in range(YB)], 1)
    v1 = [[coef_one * a + coef_naik * b for a, b in zip(x[k], p2[k])] for k in range(YB)]
    y = [vector(ys, r) for r in rows]
    q1 = [adj_vec(u(k), y[k]) for k in range(YB)]
    q1 = shift([[coef_naik * a for a in v] for v in q1], -1)
    q2 = shift([adj_vec(u(k), q1[k]) for k in range(YB)], -1)
    for k in range(YB):

        def put(c, value, k=k):
            fs[18 * d + c, rows[k], :] = value

        store_force(put, v1[k], y[k], p1[k], q1[k], x[k], q2[k])


def load_local(loads, links, ul):
    for d, mu in enumerate((1, 3)):
        for yb in range(YB):
            src, dst = links.at[mu, :, :, :, lanes(yb)], tiles(ul).at[pl.ds(18 * d, 18), yb]
            loads.start(mu, src, dst)


def local_pieces(d, first, end, ul, xs, ys, fs, sent=None):
    def body(piece, carry):
        local_piece(d, piece, (move_y, move_t)[d], ul, xs, ys, fs)
        if sent is not None:
            sent(piece)
        return carry

    lax.fori_loop(first, end, body, 0)


def first_products(ux, uz, xs, ys, pre):
    def body_z(piece, carry):
        rows = pl.ds(pl.multiple_of(piece * 8, 8), 8)
        x = [pltpu.roll(a, 7, 0) for a in vector(xs, rows)]
        y = vector(ys, rows)
        p1 = mat_vec(lambda c: uz[c, rows, :], x)
        w1 = adj_vec(lambda c: uz[c, rows, :], y)
        wx = adj_vec(lambda c: ux[c, rows, :], y)
        for c in range(6):
            pre[c, rows, :] = p1[c]
            pre[6 + c, rows, :] = coef_naik * w1[c]
            pre[18 + c, rows, :] = coef_naik * wx[c]
        return carry

    lax.fori_loop(0, ROWS // 8, body_z, 0)
    low = lax.broadcasted_iota(jnp.int32, (8, 128), 0) < CZ

    def body_x(yb, carry):
        rows = [pl.ds(pl.multiple_of(yb * CX * CZ + k * 8, 8), 8) for k in range(4)]
        half = [[pltpu.roll(a, CZ, 0) for a in vector(xs, r)] for r in rows]
        for k in range(3):
            x = [jnp.where(low, a, b) for a, b in zip(half[k], half[k + 1])]
            for c, value in enumerate(mat_vec(lambda c: ux[c, rows[k], :], x)):
                pre[12 + c, rows[k], :] = value
        return carry

    lax.fori_loop(0, YB, body_x, 0)


def early_kernel(links, ux, uz, xs, ys, _, far, xf, xb, ul, fs, pre, sem):
    def u_x(row):
        return lambda c: ux[c, pl.ds(row, 8), :]

    for yb in range(YB):
        last = yb * CX * CZ + (CX - 2) * CZ
        w1 = [coef_naik * v for v in adj_vec(u_x(last), vector(ys, pl.ds(last, 8)))]
        w2 = adj_vec(u_x(last), [pltpu.roll(v, 4, 0) for v in w1])
        for c, value in enumerate(w1 + w2):
            xb[c, yb] = value[CZ:]
        base = yb * CX * CZ
        p1 = mat_vec(u_x(base), vector(xs, pl.ds(base + CZ, 8)))
        p2 = mat_vec(u_x(base), [pltpu.roll(v, 4, 0) for v in p1])
        for c, value in enumerate(vector(xs, pl.ds(base, 8)) + p1 + p2):
            xf[c, yb] = value[:CZ]

    @pl.when(lax.axis_index("zt") == 0)
    def _():
        loads = Loads(sem)
        load_local(loads, links, ul)
        first_products(ux, uz, xs, ys, pre)
        for d, mu in enumerate((1, 3)):
            loads.wait(mu)
            local_pieces(d, 0, 4, ul, xs, ys, fs)


def local_kernel(links, ux, uz, xs, ys, _, __, ___, ul, fs, pre, force, sem, sem_out):
    first = lax.axis_index("zt") == 0
    fst = tiles(fs)

    def out_copy(piece, yb):
        return pltpu.make_async_copy(
            fst.at[pl.ds(0, 18), yb, pl.ds(2 * piece, 2)],
            force.at[1, :, pl.ds(2 * piece, 2), :, lanes(yb)],
            sem_out.at[yb * 4 + piece],
        )

    def sent(piece):
        for yb in range(YB):
            out_copy(piece, yb).start()

    @pl.when(first)
    def _():
        for piece in range(4):
            sent(piece)

    @pl.when(jnp.logical_not(first))
    def _():
        loads = Loads(sem)
        load_local(loads, links, ul)
        first_products(ux, uz, xs, ys, pre)
        loads.wait(1)
        local_pieces(0, 0, 4, ul, xs, ys, fs, sent)
        loads.wait(3)
        local_pieces(1, 0, 4, ul, xs, ys, fs)

    for yb in range(YB):
        for piece in range(4):
            out_copy(piece, yb).wait()


def edge_x_kernel(xf, xb, ux, xs, ys, pre, fz, _, force, fx, hx, sem):
    def out_copy(src, mu, yb):
        return pltpu.make_async_copy(
            tiles(src).at[:, yb], force.at[mu, :, :, :, lanes(yb)], sem.at[mu // 2 * YB + yb]
        )

    for yb in range(YB):
        out_copy(fz, 2, yb).start()
    low = lax.broadcasted_iota(jnp.int32, (8, 128), 0) < CZ
    for yb in range(YB):
        for c in range(18):
            hx[c, pl.ds(yb * 8 + CZ, CZ), :] = xf[c, yb]
        for c in range(12):
            hx[c, pl.ds(yb * 8, CZ), :] = xb[c, yb]

    def body(yb, carry):
        rows = [pl.ds(pl.multiple_of(yb * CX * CZ + k * 8, 8), 8) for k in range(4)]
        edge = pl.ds(pl.multiple_of(yb * 8, 8), 8)

        def half(vecs):
            return [[pltpu.roll(a, CZ, 0) for a in v] for v in vecs]

        def joined(r):
            return [[jnp.where(low, a, b) for a, b in zip(r[k], r[k + 1])] for k in range(4)]

        def ahead(vecs, first):
            return joined(half(vecs) + [vector(hx, edge, first)])

        def back(vecs, first):
            return joined([vector(hx, edge, first)] + half(vecs))

        def u(k):
            return lambda c: ux[c, rows[k], :]

        x = ahead([vector(xs, r) for r in rows], 0)
        p1 = ahead([vector(pre, r, 12) for r in rows[:3]] + [mat_vec(u(3), x[3])], 6)
        p2 = ahead([mat_vec(u(k), p1[k]) for k in range(4)], 12)
        v1 = [[coef_one * a + coef_naik * b for a, b in zip(x[k], p2[k])] for k in range(4)]
        y = [vector(ys, r) for r in rows]
        q1 = back([vector(pre, r, 18) for r in rows], 0)
        q2 = back([adj_vec(u(k), q1[k]) for k in range(4)], 6)
        for k in range(4):

            def put(c, value, k=k):
                fx[c, rows[k], :] = value

            store_force(put, v1[k], y[k], p1[k], q1[k], x[k], q2[k])
        out_copy(fx, 0, yb).start()
        return carry

    lax.fori_loop(0, YB, body, 0)
    for yb in range(YB):
        out_copy(fz, 2, yb).wait()
        out_copy(fx, 0, yb).wait()


def edge_z_kernel(far, near, ul, xs, ys, pre, fs, _, fz, force, hz, sem):
    def out_t(yb):
        return pltpu.make_async_copy(
            tiles(fs).at[pl.ds(18, 18), yb], force.at[3, :, :, :, lanes(yb)], sem.at[yb]
        )

    for yb in range(YB):
        out_t(yb).start()
    top_rows = pl.ds(CZ - 1, YB * CX, stride=CZ)

    def spread(zf, zb):
        p1 = mat_vec(lambda c: ul[c, top_rows, :], [zf[c] for c in range(6)])
        for c, value in enumerate([zf[c] for c in range(18)] + p1):
            hz[c, top_rows, :] = value
        for c in range(12):
            hz[c, pl.ds(0, YB * CX, stride=CZ), :] = zb[c]

    odd = lax.axis_index("zt") % 2
    pl.when(odd == 0)(lambda: spread(near, far))
    pl.when(odd == 1)(lambda: spread(far, near))
    row = lax.broadcasted_iota(jnp.int32, (8, 128), 0)
    top, bottom = row % CZ == CZ - 1, row % CZ == 0

    def body(piece, yb):
        rows = pl.ds(pl.multiple_of(yb * CX * CZ + piece * 8, 8), 8)

        def ahead(v, first):
            halo = vector(hz, rows, first)
            return [jnp.where(top, h, pltpu.roll(a, 7, 0)) for a, h in zip(v, halo)]

        def back(v, first):
            halo = vector(hz, rows, first)
            return [jnp.where(bottom, h, pltpu.roll(a, 1, 0)) for a, h in zip(v, halo)]

        def u(c):
            return ul[c, rows, :]

        x = ahead(vector(xs, rows), 0)
        own = [jnp.where(top, h, a) for a, h in zip(vector(pre, rows), vector(hz, rows, 18))]
        p1 = ahead(own, 6)
        p2 = ahead(mat_vec(u, p1), 12)
        v1 = [coef_one * a + coef_naik * b for a, b in zip(x, p2)]
        y = vector(ys, rows)
        q1 = back(vector(pre, rows, 6), 0)
        q2 = back(adj_vec(u, q1), 6)

        def put(c, value):
            fz[c, rows, :] = value

        store_force(put, v1, y, p1, q1, x, q2)
        return yb

    for yb in range(YB):
        lax.fori_loop(0, 4, body, yb)
    for yb in range(YB):
        out_t(yb).wait()


HBM = pl.BlockSpec(memory_space=pltpu.HBM)
VM = pl.BlockSpec(memory_space=pltpu.VMEM)
FORCE = jax.ShapeDtypeStruct((4, 18, CX, CZ, YT), F32)


def held(*shape):
    return pltpu.VMEM(shape, F32)


def kernel_call(body, name, flops, **args):
    return pl.pallas_call(
        body,
        name=name,
        cost_estimate=pl.CostEstimate(flops=flops, bytes_accessed=flops, transcendentals=0),
        compiler_params=pltpu.CompilerParams(vmem_limit_bytes=16 << 20),
        **args,
    )


def shifted(value, axis, step):
    size = lax.axis_size(axis)
    return lax.ppermute(value, axis, [(i, (i + step) % size) for i in range(size)])


def per_device(links, solution, product):
    links, solution, product = (
        pltpu.with_memory_space_constraint(a, pltpu.HBM) for a in (links, solution, product)
    )
    dma = pltpu.SemaphoreType.DMA
    far, near, ux, uz, xs, ys = kernel_call(
        prep_kernel,
        "prep",
        3000000,
        out_shape=(
            held(18, YB * CX, 128),
            held(20, YB * CX, 128),
            held(18, ROWS, 128),
            held(18, ROWS, 128),
            held(6, ROWS, 128),
            held(6, ROWS, 128),
        ),
        in_specs=[HBM] * 3,
        out_specs=[VM] * 6,
        scratch_shapes=[dma((12,))],
    )(links, solution, product)
    size = lax.axis_size("zt")
    near = lax.ppermute(near, "zt", [(i, i ^ 1) for i in range(size)])
    far, xf, xb, ul, fs, pre = kernel_call(
        early_kernel,
        "early",
        1000000,
        out_shape=(
            held(18, YB * CX, 128),
            held(18, YB, CZ, 128),
            held(12, YB, CZ, 128),
            held(36, ROWS, 128),
            held(36, ROWS, 128),
            held(24, ROWS, 128),
        ),
        in_specs=[HBM] + [VM] * 5,
        out_specs=[VM] * 6,
        input_output_aliases={5: 0},
        scratch_shapes=[dma((6,))],
    )(links, ux, uz, xs, ys, far)
    far = lax.ppermute(far, "zt", [(i, (i + 2 * (i % 2) - 1) % size) for i in range(size)])
    xb = shifted(xb, "xy", 1)
    xf = shifted(xf, "xy", -1)
    _, fs, pre, force = kernel_call(
        local_kernel,
        "local",
        LOCAL_COST,
        out_shape=(held(36, ROWS, 128), held(36, ROWS, 128), held(24, ROWS, 128), FORCE),
        in_specs=[HBM] + [VM] * 7,
        out_specs=[VM, VM, VM, HBM],
        input_output_aliases={5: 0, 6: 1, 7: 2},
        scratch_shapes=[dma((6,)), dma((12,))],
    )(links, ux, uz, xs, ys, ul, fs, pre)
    fz, force = kernel_call(
        edge_z_kernel,
        "edge_z",
        EDGE_Z_COST,
        out_shape=(held(18, ROWS, 128), FORCE),
        in_specs=[VM] * 7 + [HBM],
        out_specs=[VM, HBM],
        input_output_aliases={7: 1},
        scratch_shapes=[held(24, ROWS, 128), dma((3,))],
    )(far, near, uz, xs, ys, pre, fs, force)
    return kernel_call(
        edge_x_kernel,
        "edge_x",
        4000000,
        out_shape=FORCE,
        in_specs=[VM] * 7 + [HBM],
        out_specs=HBM,
        input_output_aliases={7: 0},
        scratch_shapes=[held(18, ROWS, 128), held(18, YB * 8, 128), dma((6,))],
    )(xf, xb, ux, xs, ys, pre, fz, force)


def solution(mesh):
    placed = (P(None, None, "xy", "zt", None), P(None, "xy", "zt", None), P(None, "xy", "zt", None))
    return jax.shard_map(
        per_device,
        mesh=mesh,
        in_specs=placed,
        out_specs=P(None, None, "xy", "zt", None),
        check_vma=False,
    )
```

```python
import jax
import jax.numpy as jnp
from jax import lax
from jax.experimental import pallas as pl
from jax.experimental.pallas import tpu as pltpu
from jax.sharding import PartitionSpec as P

NT = 24
CX, CZ, YT, YB = 8, 4, 384, 3
ROWS = YB * CX * CZ

coef_one = 9.0 / 8.0
coef_naik = -1.0 / 24.0

F32 = jnp.float32

LOCAL_COST = 1200000000
EDGE_Z_COST = 4000000

AHEAD = (4, 1)


def mat_vec(u, v):
    out_r, out_i = [], []
    for a in range(3):
        re = im = None
        for b in range(3):
            ur, ui = u(3 * a + b), u(9 + 3 * a + b)
            r = ur * v[b] - ui * v[3 + b]
            i = ur * v[3 + b] + ui * v[b]
            re, im = (r, i) if re is None else (re + r, im + i)
        out_r.append(re)
        out_i.append(im)
    return out_r + out_i


def adj_vec(u, v):
    out_r, out_i = [], []
    for a in range(3):
        re = im = None
        for b in range(3):
            ur, ui = u(3 * b + a), u(9 + 3 * b + a)
            r = ur * v[b] + ui * v[3 + b]
            i = ur * v[3 + b] - ui * v[b]
            re, im = (r, i) if re is None else (re + r, im + i)
        out_r.append(re)
        out_i.append(im)
    return out_r + out_i


def store_force(put, v1, y, p1, q1, x, q2):
    for a in range(3):
        for b in range(3):
            re = im = None
            for p, q in ((v1, y), (p1, q1), (x, q2)):
                r = p[a] * q[b] + p[3 + a] * q[3 + b]
                i = p[3 + a] * q[b] - p[a] * q[3 + b]
                re, im = (r, i) if re is None else (re + r, im + i)
            put(3 * a + b, re)
            put(9 + 3 * a + b, im)


def tiles(ref):
    return ref.reshape(ref.shape[0], YB, CX, CZ, 128)


def lanes(yb):
    return pl.ds(128 * yb, 128)


class Loads:
    def __init__(self, sem):
        self.sem, self.copies, self.count = sem, {}, 0

    def start(self, name, src, dst):
        copy = pltpu.make_async_copy(src, dst, self.sem.at[self.count])
        copy.start()
        self.copies.setdefault(name, []).append(copy)
        self.count += 1

    def wait(self, name):
        for copy in self.copies.pop(name):
            copy.wait()


def vector(ref, rows, first=0):
    return [ref[first + c, rows, :] for c in range(6)]


def prep_kernel(links, sol, prod, far, near, ux, uz, xs, ys, sem):
    loads = Loads(sem)
    uxt, uzt, xst, yst = tiles(ux), tiles(uz), tiles(xs), tiles(ys)
    for yb in range(YB):
        loads.start("x", sol.at[:, :, :, lanes(yb)], xst.at[:, yb])
    for yb in range(YB):
        loads.start("uz", links.at[2, :, :, :, lanes(yb)], uzt.at[:, yb])
    for yb in range(YB):
        loads.start("y", prod.at[:, :, :, lanes(yb)], yst.at[:, yb])
    for first in (0, CX - 2):
        for yb in range(YB):
            src = links.at[0, :, pl.ds(first, 2), :, lanes(yb)]
            loads.start("ux", src, uxt.at[:, yb, pl.ds(first, 2)])

    def layer(z):
        return pl.ds(z, YB * CX, stride=CZ)

    def u_z(z):
        return lambda c: uz[c, layer(z), :]

    loads.wait("x")
    loads.wait("uz")
    p1 = mat_vec(u_z(0), vector(xs, layer(1)))
    p2 = mat_vec(u_z(0), mat_vec(u_z(1), vector(xs, layer(2))))
    ahead = vector(xs, layer(0)) + p1 + p2
    loads.wait("y")
    q1 = [coef_naik * v for v in adj_vec(u_z(3), vector(ys, layer(3)))]
    q2 = adj_vec(u_z(3), [coef_naik * v for v in adj_vec(u_z(2), vector(ys, layer(2)))])
    behind = q1 + q2

    def put(to_before, to_after):
        for c, value in enumerate(ahead):
            to_before[c] = value
        for c, value in enumerate(behind):
            to_after[c] = value

    odd = lax.axis_index("zt") % 2
    pl.when(odd == 0)(lambda: put(far, near))
    pl.when(odd == 1)(lambda: put(near, far))
    loads.wait("ux")


def move_y(v, step):
    lane = lax.broadcasted_iota(jnp.int32, (8, 128), 1)
    if step > 0:
        r = [pltpu.roll(a, 128 - NT, 1) for a in v]
        return [jnp.where(lane < 128 - NT, r[k], r[(k + 1) % YB]) for k in range(YB)]
    r = [pltpu.roll(a, NT, 1) for a in v]
    return [jnp.where(lane >= NT, r[k], r[(k - 1) % YB]) for k in range(YB)]


def move_t(v, step):
    lane = lax.broadcasted_iota(jnp.int32, (8, 128), 1)
    out = []
    if step > 0:
        near = [pltpu.roll(a, 127, 1) for a in v]
        wrap = [pltpu.roll(a, NT - 1, 1) for a in v]
        for k in range(YB):
            edge = (lane + 128 * k) % NT == NT - 1
            far = wrap[k] if k == 0 else jnp.where(lane < NT - 1, wrap[k - 1], wrap[k])
            beside = near[k] if k == YB - 1 else jnp.where(lane == 127, near[k + 1], near[k])
            out.append(jnp.where(edge, far, beside))
        return out
    near = [pltpu.roll(a, 1, 1) for a in v]
    wrap = [pltpu.roll(a, 128 - (NT - 1), 1) for a in v]
    for k in range(YB):
        edge = (lane + 128 * k) % NT == 0
        far = wrap[k] if k == YB - 1 else jnp.where(lane >= 128 - (NT - 1), wrap[k + 1], wrap[k])
        beside = near[k] if k == 0 else jnp.where(lane == 0, near[k - 1], near[k])
        out.append(jnp.where(edge, far, beside))
    return out


def local_piece(d, piece, move, ul, xs, ys, fs):
    rows = [pl.ds(pl.multiple_of(yb * CX * CZ + piece * 8, 8), 8) for yb in range(YB)]

    def shift(vecs, step):
        moved = [move([vecs[k][c] for k in range(YB)], step) for c in range(6)]
        return [[moved[c][k] for c in range(6)] for k in range(YB)]

    def u(k):
        return lambda c: ul[18 * d + c, rows[k], :]

    x = shift([vector(xs, r) for r in rows], 1)
    p1 = shift([mat_vec(u(k), x[k]) for k in range(YB)], 1)
    p2 = shift([mat_vec(u(k), p1[k]) for k in range(YB)], 1)
    v1 = [[coef_one * a + coef_naik * b for a, b in zip(x[k], p2[k])] for k in range(YB)]
    y = [vector(ys, r) for r in rows]
    q1 = [adj_vec(u(k), y[k]) for k in range(YB)]
    q1 = shift([[coef_naik * a for a in v] for v in q1], -1)
    q2 = shift([adj_vec(u(k), q1[k]) for k in range(YB)], -1)
    for k in range(YB):

        def put(c, value, k=k):
            fs[18 * d + c, rows[k], :] = value

        store_force(put, v1[k], y[k], p1[k], q1[k], x[k], q2[k])


def load_local(loads, links, ux, ul):
    for yb in range(YB):
        src = links.at[0, :, pl.ds(2, CX - 4), :, lanes(yb)]
        loads.start(0, src, tiles(ux).at[:, yb, pl.ds(2, CX - 4)])
    for d, mu in enumerate((1, 3)):
        for yb in range(YB):
            src, dst = links.at[mu, :, :, :, lanes(yb)], tiles(ul).at[pl.ds(18 * d, 18), yb]
            loads.start(mu, src, dst)


def local_pieces(d, first, end, ul, xs, ys, fs, sent=None):
    def body(piece, carry):
        local_piece(d, piece, (move_y, move_t)[d], ul, xs, ys, fs)
        if sent is not None:
            sent(piece)
        return carry

    lax.fori_loop(first, end, body, 0)


def slices(yb):
    return [pl.ds(pl.multiple_of(yb * CX * CZ + k * 8, 8), 8) for k in range(4)]


def halves(vec):
    return [pltpu.roll(a, CZ, 0) for a in vec]


def joined(first, second):
    low = lax.broadcasted_iota(jnp.int32, (8, 128), 0) < CZ
    return [jnp.where(low, a, b) for a, b in zip(first, second)]


def scaled(vec):
    return [coef_naik * a for a in vec]


def mixed(x, p2):
    return [coef_one * a + coef_naik * b for a, b in zip(x, p2)]


def first_products(loads, ux, uz, xs, ys, pre, fx):
    def body_z(piece, carry):
        rows = pl.ds(pl.multiple_of(piece * 8, 8), 8)
        p1 = mat_vec(lambda c: uz[c, rows, :], [pltpu.roll(a, 7, 0) for a in vector(xs, rows)])
        w1 = scaled(adj_vec(lambda c: uz[c, rows, :], vector(ys, rows)))
        for c, value in enumerate(p1 + w1):
            pre[c, rows, :] = value
        return carry

    lax.fori_loop(0, ROWS // 8, body_z, 0)
    loads.wait(0)

    def body_x(yb, carry):
        rows = slices(yb)

        def u(k):
            return lambda c: ux[c, rows[k], :]

        def keep(k, vecs):
            for c, value in enumerate(sum(vecs, [])):
                pre[12 + c, rows[k], :] = value

        y = [vector(ys, r) for r in rows]
        h = [halves(vector(xs, r)) for r in rows]
        x = [joined(h[k], h[k + 1]) for k in range(3)]
        p1_raw = [mat_vec(u(k), x[k]) for k in range(3)]
        h = [halves(v) for v in p1_raw]
        p1 = [joined(h[0], h[1]), joined(h[1], h[2]), h[2]]
        h = [halves(mat_vec(u(k), p1[k])) for k in range(3)]
        v1 = [mixed(x[k], joined(h[k], h[k + 1])) for k in range(2)]
        w1 = [scaled(adj_vec(u(k), y[k])) for k in range(4)]
        h = [halves(v) for v in w1]
        q1 = [h[0]] + [joined(h[k - 1], h[k]) for k in (1, 2, 3)]
        h = [halves(adj_vec(u(k), q1[k])) for k in range(4)]
        q2 = [None] + [joined(h[k - 1], h[k]) for k in (1, 2, 3)]
        keep(0, [v1[0], p1[0], x[0], w1[0]])
        keep(2, [q1[2], q2[2], p1_raw[2]])
        keep(3, [q1[3], q2[3]])

        def put(c, value):
            fx[c, rows[1], :] = value

        store_force(put, v1[1], y[1], p1[1], q1[1], x[1], q2[1])
        return carry

    lax.fori_loop(0, YB, body_x, 0)


def early_kernel(links, uz, xs, ys, _, __, far, ux, xf, xb, ul, fs, pre, fx, sem):
    def u_x(row):
        return lambda c: ux[c, pl.ds(row, 8), :]

    for yb in range(YB):
        last = yb * CX * CZ + (CX - 2) * CZ
        w1 = [coef_naik * v for v in adj_vec(u_x(last), vector(ys, pl.ds(last, 8)))]
        w2 = adj_vec(u_x(last), [pltpu.roll(v, 4, 0) for v in w1])
        for c, value in enumerate(w1 + w2):
            xb[c, yb] = value[CZ:]
        base = yb * CX * CZ
        p1 = mat_vec(u_x(base), vector(xs, pl.ds(base + CZ, 8)))
        p2 = mat_vec(u_x(base), [pltpu.roll(v, 4, 0) for v in p1])
        for c, value in enumerate(vector(xs, pl.ds(base, 8)) + p1 + p2):
            xf[c, yb] = value[:CZ]

    @pl.when(lax.axis_index("zt") == 0)
    def _():
        loads = Loads(sem)
        load_local(loads, links, ux, ul)
        first_products(loads, ux, uz, xs, ys, pre, fx)
        for d, mu in enumerate((1, 3)):
            loads.wait(mu)
            local_pieces(d, 0, AHEAD[d], ul, xs, ys, fs)


def local_kernel(links, uz, xs, ys, *refs):
    ux, ul, fs, pre, fx, force, sem, sem_out = refs[5:]
    first = lax.axis_index("zt") == 0
    fst = tiles(fs)

    def out_copy(piece, yb):
        return pltpu.make_async_copy(
            fst.at[pl.ds(0, 18), yb, pl.ds(2 * piece, 2)],
            force.at[1, :, pl.ds(2 * piece, 2), :, lanes(yb)],
            sem_out.at[yb * 4 + piece],
        )

    def sent(piece):
        for yb in range(YB):
            out_copy(piece, yb).start()

    @pl.when(first)
    def _():
        for piece in range(AHEAD[0]):
            sent(piece)
        local_pieces(0, AHEAD[0], 4, ul, xs, ys, fs, sent)
        local_pieces(1, AHEAD[1], 4, ul, xs, ys, fs)

    @pl.when(jnp.logical_not(first))
    def _():
        loads = Loads(sem)
        load_local(loads, links, ux, ul)
        first_products(loads, ux, uz, xs, ys, pre, fx)
        loads.wait(1)
        local_pieces(0, 0, 4, ul, xs, ys, fs, sent)
        loads.wait(3)
        local_pieces(1, 0, 4, ul, xs, ys, fs)

    for yb in range(YB):
        for piece in range(4):
            out_copy(piece, yb).wait()


def edge_back_kernel(xb, ux, ys, pre, _, __, fx, force, hx):
    for yb in range(YB):
        for c in range(12):
            hx[c, pl.ds(yb * 8, CZ), :] = xb[c, yb]
    for yb in range(YB):
        rows = slices(yb)[0]
        edge = pl.ds(yb * 8, 8)
        q1 = joined(vector(hx, edge), halves(vector(pre, rows, 30)))
        w2 = adj_vec(lambda c: ux[c, rows, :], q1)
        q2 = joined(vector(hx, edge, 6), halves(w2))

        def put(c, value):
            fx[c, rows, :] = value

        v1, p1, x = (vector(pre, rows, first) for first in (12, 18, 24))
        store_force(put, v1, vector(ys, rows), p1, q1, x, q2)


def edge_ahead_kernel(xf, ux, xs, ys, pre, fx, _, force, f2, hx, sem):
    def out_copy(src, first, yb):
        return pltpu.make_async_copy(
            tiles(src).at[:, yb, pl.ds(first, CX // 2)],
            force.at[0, :, pl.ds(first, CX // 2), :, lanes(yb)],
            sem.at[first // 4 * YB + yb],
        )

    for yb in range(YB):
        out_copy(fx, 0, yb).start()
        for c in range(18):
            hx[c, pl.ds(yb * 8 + CZ, CZ), :] = xf[c, yb]
    for yb in range(YB):
        rows = slices(yb)
        edge = pl.ds(yb * 8, 8)

        def u(k):
            return lambda c: ux[c, rows[k], :]

        def ahead(second, third, first):
            h = [halves(second), halves(third), vector(hx, edge, first)]
            return {2: joined(h[0], h[1]), 3: joined(h[1], h[2])}

        x = ahead(vector(xs, rows[2]), vector(xs, rows[3]), 0)
        p1 = ahead(vector(pre, rows[2], 24), mat_vec(u(3), x[3]), 6)
        p2 = ahead(mat_vec(u(2), p1[2]), mat_vec(u(3), p1[3]), 12)
        for k in (2, 3):

            def put(c, value, k=k):
                f2[c, rows[k], :] = value

            q1, q2 = vector(pre, rows[k], 12), vector(pre, rows[k], 18)
            store_force(put, mixed(x[k], p2[k]), vector(ys, rows[k]), p1[k], q1, x[k], q2)
        out_copy(f2, CX // 2, yb).start()
    for first, src in ((0, fx), (CX // 2, f2)):
        for yb in range(YB):
            out_copy(src, first, yb).wait()


def edge_z_kernel(far, near, ul, xs, ys, pre, fs, _, force, fz, hz, sem):
    def out_t(yb):
        return pltpu.make_async_copy(
            tiles(fs).at[pl.ds(18, 18), yb], force.at[3, :, :, :, lanes(yb)], sem.at[yb]
        )

    def out_z(yb):
        return pltpu.make_async_copy(
            tiles(fz).at[:, yb], force.at[2, :, :, :, lanes(yb)], sem.at[YB + yb]
        )

    for yb in range(YB):
        out_t(yb).start()
    top_rows = pl.ds(CZ - 1, YB * CX, stride=CZ)

    def spread(zf, zb):
        p1 = mat_vec(lambda c: ul[c, top_rows, :], [zf[c] for c in range(6)])
        for c, value in enumerate([zf[c] for c in range(18)] + p1):
            hz[c, top_rows, :] = value
        for c in range(12):
            hz[c, pl.ds(0, YB * CX, stride=CZ), :] = zb[c]

    odd = lax.axis_index("zt") % 2
    pl.when(odd == 0)(lambda: spread(near, far))
    pl.when(odd == 1)(lambda: spread(far, near))
    row = lax.broadcasted_iota(jnp.int32, (8, 128), 0)
    top, bottom = row % CZ == CZ - 1, row % CZ == 0

    def body(piece, yb):
        rows = pl.ds(pl.multiple_of(yb * CX * CZ + piece * 8, 8), 8)

        def ahead(v, first):
            halo = vector(hz, rows, first)
            return [jnp.where(top, h, pltpu.roll(a, 7, 0)) for a, h in zip(v, halo)]

        def back(v, first):
            halo = vector(hz, rows, first)
            return [jnp.where(bottom, h, pltpu.roll(a, 1, 0)) for a, h in zip(v, halo)]

        def u(c):
            return ul[c, rows, :]

        x = ahead(vector(xs, rows), 0)
        own = [jnp.where(top, h, a) for a, h in zip(vector(pre, rows), vector(hz, rows, 18))]
        p1 = ahead(own, 6)
        p2 = ahead(mat_vec(u, p1), 12)
        v1 = [coef_one * a + coef_naik * b for a, b in zip(x, p2)]
        y = vector(ys, rows)
        q1 = back(vector(pre, rows, 6), 0)
        q2 = back(adj_vec(u, q1), 6)

        def put(c, value):
            fz[c, rows, :] = value

        store_force(put, v1, y, p1, q1, x, q2)
        return yb

    for yb in range(YB):
        lax.fori_loop(0, 4, body, yb)
        out_z(yb).start()
    for yb in range(YB):
        out_t(yb).wait()
        out_z(yb).wait()


HBM = pl.BlockSpec(memory_space=pltpu.HBM)
VM = pl.BlockSpec(memory_space=pltpu.VMEM)
FORCE = jax.ShapeDtypeStruct((4, 18, CX, CZ, YT), F32)


def held(*shape):
    return pltpu.VMEM(shape, F32)


def kernel_call(body, name, flops, **args):
    return pl.pallas_call(
        body,
        name=name,
        cost_estimate=pl.CostEstimate(flops=flops, bytes_accessed=flops, transcendentals=0),
        compiler_params=pltpu.CompilerParams(vmem_limit_bytes=16 << 20),
        **args,
    )


def shifted(value, axis, step):
    size = lax.axis_size(axis)
    return lax.ppermute(value, axis, [(i, (i + step) % size) for i in range(size)])


def per_device(links, solution, product):
    links, solution, product = (
        pltpu.with_memory_space_constraint(a, pltpu.HBM) for a in (links, solution, product)
    )
    dma = pltpu.SemaphoreType.DMA
    far, near, ux, uz, xs, ys = kernel_call(
        prep_kernel,
        "prep",
        3000000,
        out_shape=(
            held(18, YB * CX, 128),
            held(20, YB * CX, 128),
            held(18, ROWS, 128),
            held(18, ROWS, 128),
            held(6, ROWS, 128),
            held(6, ROWS, 128),
        ),
        in_specs=[HBM] * 3,
        out_specs=[VM] * 6,
        scratch_shapes=[dma((15,))],
    )(links, solution, product)
    size = lax.axis_size("zt")
    near = lax.ppermute(near, "zt", [(i, i ^ 1) for i in range(size)])
    far, ux, xf, xb, *work = kernel_call(
        early_kernel,
        "early",
        1000000,
        out_shape=(
            held(18, YB * CX, 128),
            held(18, ROWS, 128),
            held(18, YB, CZ, 128),
            held(12, YB, CZ, 128),
            held(36, ROWS, 128),
            held(36, ROWS, 128),
            held(36, ROWS, 128),
            held(18, ROWS, 128),
        ),
        in_specs=[HBM] + [VM] * 5,
        out_specs=[VM] * 8,
        input_output_aliases={4: 0, 5: 1},
        scratch_shapes=[dma((9,))],
    )(links, uz, xs, ys, far, ux)
    far = lax.ppermute(far, "zt", [(i, (i + 2 * (i % 2) - 1) % size) for i in range(size)])
    xb = shifted(xb, "xy", 1)
    xf = shifted(xf, "xy", -1)
    ux, _, fs, pre, fx, force = kernel_call(
        local_kernel,
        "local",
        LOCAL_COST,
        out_shape=(
            held(18, ROWS, 128),
            held(36, ROWS, 128),
            held(36, ROWS, 128),
            held(36, ROWS, 128),
            held(18, ROWS, 128),
            FORCE,
        ),
        in_specs=[HBM] + [VM] * 8,
        out_specs=[VM] * 5 + [HBM],
        input_output_aliases={4: 0, 5: 1, 6: 2, 7: 3, 8: 4},
        scratch_shapes=[dma((9,)), dma((12,))],
    )(links, uz, xs, ys, ux, *work)
    force = kernel_call(
        edge_z_kernel,
        "edge_z",
        EDGE_Z_COST,
        out_shape=FORCE,
        in_specs=[VM] * 7 + [HBM],
        out_specs=HBM,
        input_output_aliases={7: 0},
        scratch_shapes=[held(18, ROWS, 128), held(24, ROWS, 128), dma((6,))],
    )(far, near, uz, xs, ys, pre, fs, force)
    fx, force = kernel_call(
        edge_back_kernel,
        "edge_back",
        4000000,
        out_shape=(held(18, ROWS, 128), FORCE),
        in_specs=[VM] * 5 + [HBM],
        out_specs=[VM, HBM],
        input_output_aliases={4: 0, 5: 1},
        scratch_shapes=[held(12, YB * 8, 128)],
    )(xb, ux, ys, pre, fx, force)
    return kernel_call(
        edge_ahead_kernel,
        "edge_ahead",
        4000000,
        out_shape=FORCE,
        in_specs=[VM] * 6 + [HBM],
        out_specs=HBM,
        input_output_aliases={6: 0},
        scratch_shapes=[held(18, ROWS, 128), held(18, YB * 8, 128), dma((6,))],
    )(xf, ux, xs, ys, pre, fx, force)


def solution(mesh):
    placed = (P(None, None, "xy", "zt", None), P(None, "xy", "zt", None), P(None, "xy", "zt", None))
    return jax.shard_map(
        per_device,
        mesh=mesh,
        in_specs=placed,
        out_specs=P(None, None, "xy", "zt", None),
        check_vma=False,
    )
```

```python
import jax
import jax.numpy as jnp
from jax import lax
from jax.experimental import pallas as pl
from jax.experimental.pallas import tpu as pltpu
from jax.sharding import PartitionSpec as P

NT = 24
CX, CZ, YT, YB = 8, 4, 384, 3
ROWS = YB * CX * CZ

coef_one = 9.0 / 8.0
coef_naik = -1.0 / 24.0

F32 = jnp.float32

LOCAL_COST = 1000000
EDGE_Z_COST = 4000000
EDGE_BACK_COST = 2000000000

AHEAD = (2, 0)


def mat_vec(u, v):
    out_r, out_i = [], []
    for a in range(3):
        re = im = None
        for b in range(3):
            ur, ui = u(3 * a + b), u(9 + 3 * a + b)
            r = ur * v[b] - ui * v[3 + b]
            i = ur * v[3 + b] + ui * v[b]
            re, im = (r, i) if re is None else (re + r, im + i)
        out_r.append(re)
        out_i.append(im)
    return out_r + out_i


def adj_vec(u, v):
    out_r, out_i = [], []
    for a in range(3):
        re = im = None
        for b in range(3):
            ur, ui = u(3 * b + a), u(9 + 3 * b + a)
            r = ur * v[b] + ui * v[3 + b]
            i = ur * v[3 + b] - ui * v[b]
            re, im = (r, i) if re is None else (re + r, im + i)
        out_r.append(re)
        out_i.append(im)
    return out_r + out_i


def store_force(put, v1, y, p1, q1, x, q2):
    for a in range(3):
        for b in range(3):
            re = im = None
            for p, q in ((v1, y), (p1, q1), (x, q2)):
                r = p[a] * q[b] + p[3 + a] * q[3 + b]
                i = p[3 + a] * q[b] - p[a] * q[3 + b]
                re, im = (r, i) if re is None else (re + r, im + i)
            put(3 * a + b, re)
            put(9 + 3 * a + b, im)


def tiles(ref):
    return ref.reshape(ref.shape[0], YB, CX, CZ, 128)


def lanes(yb):
    return pl.ds(128 * yb, 128)


class Loads:
    def __init__(self, sem):
        self.sem, self.copies, self.count = sem, {}, 0

    def start(self, name, src, dst):
        copy = pltpu.make_async_copy(src, dst, self.sem.at[self.count])
        copy.start()
        self.copies.setdefault(name, []).append(copy)
        self.count += 1

    def wait(self, name):
        for copy in self.copies.pop(name):
            copy.wait()


def vector(ref, rows, first=0):
    return [ref[first + c, rows, :] for c in range(6)]


def prep_kernel(links, sol, prod, far, near, xf, xb, ux, uz, xs, ys, sem):
    loads = Loads(sem)
    uxt, uzt, xst, yst = tiles(ux), tiles(uz), tiles(xs), tiles(ys)
    for yb in range(YB):
        loads.start("x", sol.at[:, :, :, lanes(yb)], xst.at[:, yb])
    for yb in range(YB):
        loads.start("uz", links.at[2, :, :, :, lanes(yb)], uzt.at[:, yb])
    for yb in range(YB):
        loads.start("y", prod.at[:, :, :, lanes(yb)], yst.at[:, yb])
    for first in (0, CX - 2):
        for yb in range(YB):
            src = links.at[0, :, pl.ds(first, 2), :, lanes(yb)]
            loads.start("ux", src, uxt.at[:, yb, pl.ds(first, 2)])

    def layer(z):
        return pl.ds(z, YB * CX, stride=CZ)

    def u_z(z):
        return lambda c: uz[c, layer(z), :]

    loads.wait("x")
    loads.wait("uz")
    p1 = mat_vec(u_z(0), vector(xs, layer(1)))
    p2 = mat_vec(u_z(0), mat_vec(u_z(1), vector(xs, layer(2))))
    ahead = vector(xs, layer(0)) + p1 + p2
    loads.wait("y")
    q1 = [coef_naik * v for v in adj_vec(u_z(3), vector(ys, layer(3)))]
    q2 = adj_vec(u_z(3), [coef_naik * v for v in adj_vec(u_z(2), vector(ys, layer(2)))])
    behind = q1 + q2

    def put(to_before, to_after):
        for c, value in enumerate(ahead):
            to_before[c] = value
        for c, value in enumerate(behind):
            to_after[c] = value

    odd = lax.axis_index("zt") % 2
    pl.when(odd == 0)(lambda: put(far, near))
    pl.when(odd == 1)(lambda: put(near, far))
    loads.wait("ux")

    def u_x(row):
        return lambda c: ux[c, pl.ds(row, 8), :]

    for yb in range(YB):
        last = yb * CX * CZ + (CX - 2) * CZ
        w1 = [coef_naik * v for v in adj_vec(u_x(last), vector(ys, pl.ds(last, 8)))]
        w2 = adj_vec(u_x(last), [pltpu.roll(v, 4, 0) for v in w1])
        for c, value in enumerate(w1 + w2):
            xb[c, yb] = value[CZ:]
        base = yb * CX * CZ
        p1 = mat_vec(u_x(base), vector(xs, pl.ds(base + CZ, 8)))
        p2 = mat_vec(u_x(base), [pltpu.roll(v, 4, 0) for v in p1])
        for c, value in enumerate(vector(xs, pl.ds(base, 8)) + p1 + p2):
            xf[c, yb] = value[:CZ]


def move_y(v, step):
    lane = lax.broadcasted_iota(jnp.int32, (8, 128), 1)
    if step > 0:
        r = [pltpu.roll(a, 128 - NT, 1) for a in v]
        return [jnp.where(lane < 128 - NT, r[k], r[(k + 1) % YB]) for k in range(YB)]
    r = [pltpu.roll(a, NT, 1) for a in v]
    return [jnp.where(lane >= NT, r[k], r[(k - 1) % YB]) for k in range(YB)]


def move_t(v, step):
    lane = lax.broadcasted_iota(jnp.int32, (8, 128), 1)
    out = []
    if step > 0:
        near = [pltpu.roll(a, 127, 1) for a in v]
        wrap = [pltpu.roll(a, NT - 1, 1) for a in v]
        for k in range(YB):
            edge = (lane + 128 * k) % NT == NT - 1
            far = wrap[k] if k == 0 else jnp.where(lane < NT - 1, wrap[k - 1], wrap[k])
            beside = near[k] if k == YB - 1 else jnp.where(lane == 127, near[k + 1], near[k])
            out.append(jnp.where(edge, far, beside))
        return out
    near = [pltpu.roll(a, 1, 1) for a in v]
    wrap = [pltpu.roll(a, 128 - (NT - 1), 1) for a in v]
    for k in range(YB):
        edge = (lane + 128 * k) % NT == 0
        far = wrap[k] if k == YB - 1 else jnp.where(lane >= 128 - (NT - 1), wrap[k + 1], wrap[k])
        beside = near[k] if k == 0 else jnp.where(lane == 0, near[k - 1], near[k])
        out.append(jnp.where(edge, far, beside))
    return out


def local_piece(d, piece, move, ul, xs, ys, fs):
    rows = [pl.ds(pl.multiple_of(yb * CX * CZ + piece * 8, 8), 8) for yb in range(YB)]

    def shift(vecs, step):
        moved = [move([vecs[k][c] for k in range(YB)], step) for c in range(6)]
        return [[moved[c][k] for c in range(6)] for k in range(YB)]

    def u(k):
        return lambda c: ul[18 * d + c, rows[k], :]

    x = shift([vector(xs, r) for r in rows], 1)
    p1 = shift([mat_vec(u(k), x[k]) for k in range(YB)], 1)
    p2 = shift([mat_vec(u(k), p1[k]) for k in range(YB)], 1)
    v1 = [[coef_one * a + coef_naik * b for a, b in zip(x[k], p2[k])] for k in range(YB)]
    y = [vector(ys, r) for r in rows]
    q1 = [adj_vec(u(k), y[k]) for k in range(YB)]
    q1 = shift([[coef_naik * a for a in v] for v in q1], -1)
    q2 = shift([adj_vec(u(k), q1[k]) for k in range(YB)], -1)
    for k in range(YB):

        def put(c, value, k=k):
            fs[18 * d + c, rows[k], :] = value

        store_force(put, v1[k], y[k], p1[k], q1[k], x[k], q2[k])


def load_local(loads, links, ux, ul):
    for yb in range(YB):
        src = links.at[0, :, pl.ds(2, CX - 4), :, lanes(yb)]
        loads.start(0, src, tiles(ux).at[:, yb, pl.ds(2, CX - 4)])
    for d, mu in enumerate((1, 3)):
        for yb in range(YB):
            src, dst = links.at[mu, :, :, :, lanes(yb)], tiles(ul).at[pl.ds(18 * d, 18), yb]
            loads.start(mu, src, dst)


def local_pieces(d, first, end, ul, xs, ys, fs, sent=None):
    def body(piece, carry):
        local_piece(d, piece, (move_y, move_t)[d], ul, xs, ys, fs)
        if sent is not None:
            sent(piece)
        return carry

    lax.fori_loop(first, end, body, 0)


def slices(yb):
    return [pl.ds(pl.multiple_of(yb * CX * CZ + k * 8, 8), 8) for k in range(4)]


def halves(vec):
    return [pltpu.roll(a, CZ, 0) for a in vec]


def joined(first, second):
    low = lax.broadcasted_iota(jnp.int32, (8, 128), 0) < CZ
    return [jnp.where(low, a, b) for a, b in zip(first, second)]


def scaled(vec):
    return [coef_naik * a for a in vec]


def mixed(x, p2):
    return [coef_one * a + coef_naik * b for a, b in zip(x, p2)]


def first_products(loads, ux, uz, xs, ys, pre, fx):
    def body_z(piece, carry):
        rows = pl.ds(pl.multiple_of(piece * 8, 8), 8)
        p1 = mat_vec(lambda c: uz[c, rows, :], [pltpu.roll(a, 7, 0) for a in vector(xs, rows)])
        w1 = scaled(adj_vec(lambda c: uz[c, rows, :], vector(ys, rows)))
        for c, value in enumerate(p1 + w1):
            pre[c, rows, :] = value
        return carry

    lax.fori_loop(0, ROWS // 8, body_z, 0)
    loads.wait(0)

    def body_x(yb, carry):
        rows = slices(yb)

        def u(k):
            return lambda c: ux[c, rows[k], :]

        def keep(k, vecs):
            for c, value in enumerate(sum(vecs, [])):
                pre[12 + c, rows[k], :] = value

        y = [vector(ys, r) for r in rows]
        h = [halves(vector(xs, r)) for r in rows]
        x = [joined(h[k], h[k + 1]) for k in range(3)]
        p1_raw = [mat_vec(u(k), x[k]) for k in range(3)]
        h = [halves(v) for v in p1_raw]
        p1 = [joined(h[0], h[1]), joined(h[1], h[2]), h[2]]
        h = [halves(mat_vec(u(k), p1[k])) for k in range(3)]
        v1 = [mixed(x[k], joined(h[k], h[k + 1])) for k in range(2)]
        w1 = [scaled(adj_vec(u(k), y[k])) for k in range(4)]
        h = [halves(v) for v in w1]
        q1 = [h[0]] + [joined(h[k - 1], h[k]) for k in (1, 2, 3)]
        h = [halves(adj_vec(u(k), q1[k])) for k in range(4)]
        q2 = [None] + [joined(h[k - 1], h[k]) for k in (1, 2, 3)]
        keep(0, [v1[0], p1[0], x[0], w1[0]])
        keep(2, [q1[2], q2[2], p1_raw[2]])
        keep(3, [q1[3], q2[3]])

        def put(c, value):
            fx[c, rows[1], :] = value

        store_force(put, v1[1], y[1], p1[1], q1[1], x[1], q2[1])
        return carry

    lax.fori_loop(0, YB, body_x, 0)


def early_kernel(links, uz, xs, ys, _, __, far, ux, ul, fs, pre, fx, sem):
    @pl.when(lax.axis_index("zt") == 0)
    def _():
        loads = Loads(sem)
        load_local(loads, links, ux, ul)
        first_products(loads, ux, uz, xs, ys, pre, fx)
        for d, mu in enumerate((1, 3)):
            loads.wait(mu)
            local_pieces(d, 0, AHEAD[d], ul, xs, ys, fs)


def local_kernel(links, uz, xs, ys, *refs):
    ux, ul, fs, pre, fx, force, sem, sem_out = refs[5:]
    first = lax.axis_index("zt") == 0
    fst = tiles(fs)

    def out_copy(piece, yb):
        return pltpu.make_async_copy(
            fst.at[pl.ds(0, 18), yb, pl.ds(2 * piece, 2)],
            force.at[1, :, pl.ds(2 * piece, 2), :, lanes(yb)],
            sem_out.at[yb * 4 + piece],
        )

    def sent(piece):
        for yb in range(YB):
            out_copy(piece, yb).start()

    @pl.when(first)
    def _():
        for piece in range(AHEAD[0]):
            sent(piece)
        local_pieces(0, AHEAD[0], 4, ul, xs, ys, fs, sent)
        local_pieces(1, AHEAD[1], 4, ul, xs, ys, fs)

    @pl.when(jnp.logical_not(first))
    def _():
        loads = Loads(sem)
        load_local(loads, links, ux, ul)
        first_products(loads, ux, uz, xs, ys, pre, fx)
        loads.wait(1)
        local_pieces(0, 0, 4, ul, xs, ys, fs, sent)
        loads.wait(3)
        local_pieces(1, 0, 4, ul, xs, ys, fs)

    for yb in range(YB):
        for piece in range(4):
            out_copy(piece, yb).wait()


def edge_back_kernel(xb, ux, ys, pre, _, __, fx, force, hx):
    for yb in range(YB):
        for c in range(12):
            hx[c, pl.ds(yb * 8, CZ), :] = xb[c, yb]
    for yb in range(YB):
        rows = slices(yb)[0]
        edge = pl.ds(yb * 8, 8)
        q1 = joined(vector(hx, edge), halves(vector(pre, rows, 30)))
        w2 = adj_vec(lambda c: ux[c, rows, :], q1)
        q2 = joined(vector(hx, edge, 6), halves(w2))

        def put(c, value):
            fx[c, rows, :] = value

        v1, p1, x = (vector(pre, rows, first) for first in (12, 18, 24))
        store_force(put, v1, vector(ys, rows), p1, q1, x, q2)


def edge_ahead_kernel(xf, ux, xs, ys, pre, fx, fz, _, force, f2, hx, sem):
    for yb in range(1, YB):
        out_z(fz, force, yb, sem.at[2 * YB + yb - 1]).start()

    def out_copy(src, first, yb):
        return pltpu.make_async_copy(
            tiles(src).at[:, yb, pl.ds(first, CX // 2)],
            force.at[0, :, pl.ds(first, CX // 2), :, lanes(yb)],
            sem.at[first // 4 * YB + yb],
        )

    for yb in range(YB):
        out_copy(fx, 0, yb).start()
        for c in range(18):
            hx[c, pl.ds(yb * 8 + CZ, CZ), :] = xf[c, yb]
    for yb in range(YB):
        rows = slices(yb)
        edge = pl.ds(yb * 8, 8)

        def u(k):
            return lambda c: ux[c, rows[k], :]

        def ahead(second, third, first):
            h = [halves(second), halves(third), vector(hx, edge, first)]
            return {2: joined(h[0], h[1]), 3: joined(h[1], h[2])}

        x = ahead(vector(xs, rows[2]), vector(xs, rows[3]), 0)
        p1 = ahead(vector(pre, rows[2], 24), mat_vec(u(3), x[3]), 6)
        p2 = ahead(mat_vec(u(2), p1[2]), mat_vec(u(3), p1[3]), 12)
        for k in (2, 3):

            def put(c, value, k=k):
                f2[c, rows[k], :] = value

            q1, q2 = vector(pre, rows[k], 12), vector(pre, rows[k], 18)
            store_force(put, mixed(x[k], p2[k]), vector(ys, rows[k]), p1[k], q1, x[k], q2)
        out_copy(f2, CX // 2, yb).start()
    for first, src in ((0, fx), (CX // 2, f2)):
        for yb in range(YB):
            out_copy(src, first, yb).wait()
    for yb in range(1, YB):
        out_z(fz, force, yb, sem.at[2 * YB + yb - 1]).wait()


def out_z(fz, force, yb, sem):
    return pltpu.make_async_copy(tiles(fz).at[:, yb], force.at[2, :, :, :, lanes(yb)], sem)


def edge_z_kernel(far, near, ul, xs, ys, pre, fs, _, fz, force, hz, sem):
    def out_t(yb):
        return pltpu.make_async_copy(
            tiles(fs).at[pl.ds(18, 18), yb], force.at[3, :, :, :, lanes(yb)], sem.at[yb]
        )

    for yb in range(YB):
        out_t(yb).start()
    top_rows = pl.ds(CZ - 1, YB * CX, stride=CZ)

    def spread(zf, zb):
        p1 = mat_vec(lambda c: ul[c, top_rows, :], [zf[c] for c in range(6)])
        for c, value in enumerate([zf[c] for c in range(18)] + p1):
            hz[c, top_rows, :] = value
        for c in range(12):
            hz[c, pl.ds(0, YB * CX, stride=CZ), :] = zb[c]

    odd = lax.axis_index("zt") % 2
    pl.when(odd == 0)(lambda: spread(near, far))
    pl.when(odd == 1)(lambda: spread(far, near))
    row = lax.broadcasted_iota(jnp.int32, (8, 128), 0)
    top, bottom = row % CZ == CZ - 1, row % CZ == 0

    def body(piece, yb):
        rows = pl.ds(pl.multiple_of(yb * CX * CZ + piece * 8, 8), 8)

        def ahead(v, first):
            halo = vector(hz, rows, first)
            return [jnp.where(top, h, pltpu.roll(a, 7, 0)) for a, h in zip(v, halo)]

        def back(v, first):
            halo = vector(hz, rows, first)
            return [jnp.where(bottom, h, pltpu.roll(a, 1, 0)) for a, h in zip(v, halo)]

        def u(c):
            return ul[c, rows, :]

        x = ahead(vector(xs, rows), 0)
        own = [jnp.where(top, h, a) for a, h in zip(vector(pre, rows), vector(hz, rows, 18))]
        p1 = ahead(own, 6)
        p2 = ahead(mat_vec(u, p1), 12)
        v1 = [coef_one * a + coef_naik * b for a, b in zip(x, p2)]
        y = vector(ys, rows)
        q1 = back(vector(pre, rows, 6), 0)
        q2 = back(adj_vec(u, q1), 6)

        def put(c, value):
            fz[c, rows, :] = value

        store_force(put, v1, y, p1, q1, x, q2)
        return yb

    for yb in range(YB):
        lax.fori_loop(0, 4, body, yb)
        if yb == 0:
            out_z(fz, force, yb, sem.at[YB]).start()
    for yb in range(YB):
        out_t(yb).wait()
    out_z(fz, force, 0, sem.at[YB]).wait()


HBM = pl.BlockSpec(memory_space=pltpu.HBM)
VM = pl.BlockSpec(memory_space=pltpu.VMEM)
FORCE = jax.ShapeDtypeStruct((4, 18, CX, CZ, YT), F32)


def held(*shape):
    return pltpu.VMEM(shape, F32)


def kernel_call(body, name, flops, **args):
    return pl.pallas_call(
        body,
        name=name,
        cost_estimate=pl.CostEstimate(flops=flops, bytes_accessed=flops, transcendentals=0),
        compiler_params=pltpu.CompilerParams(vmem_limit_bytes=16 << 20),
        **args,
    )


def shifted(value, axis, step):
    size = lax.axis_size(axis)
    return lax.ppermute(value, axis, [(i, (i + step) % size) for i in range(size)])


def per_device(links, solution, product):
    links, solution, product = (
        pltpu.with_memory_space_constraint(a, pltpu.HBM) for a in (links, solution, product)
    )
    dma = pltpu.SemaphoreType.DMA
    far, near, xf, xb, ux, uz, xs, ys = kernel_call(
        prep_kernel,
        "prep",
        3000000,
        out_shape=(
            held(18, YB * CX, 128),
            held(20, YB * CX, 128),
            held(18, YB, CZ, 128),
            held(12, YB, CZ, 128),
            held(18, ROWS, 128),
            held(18, ROWS, 128),
            held(6, ROWS, 128),
            held(6, ROWS, 128),
        ),
        in_specs=[HBM] * 3,
        out_specs=[VM] * 8,
        scratch_shapes=[dma((15,))],
    )(links, solution, product)
    size = lax.axis_size("zt")
    near = lax.ppermute(near, "zt", [(i, i ^ 1) for i in range(size)])
    far, ux, *work = kernel_call(
        early_kernel,
        "early",
        1000000,
        out_shape=(
            held(18, YB * CX, 128),
            held(18, ROWS, 128),
            held(36, ROWS, 128),
            held(36, ROWS, 128),
            held(36, ROWS, 128),
            held(18, ROWS, 128),
        ),
        in_specs=[HBM] + [VM] * 5,
        out_specs=[VM] * 6,
        input_output_aliases={4: 0, 5: 1},
        scratch_shapes=[dma((9,))],
    )(links, uz, xs, ys, far, ux)
    far = lax.ppermute(far, "zt", [(i, (i + 2 * (i % 2) - 1) % size) for i in range(size)])
    xb = shifted(xb, "xy", 1)
    xf = shifted(xf, "xy", -1)
    ux, _, fs, pre, fx, force = kernel_call(
        local_kernel,
        "local",
        LOCAL_COST,
        out_shape=(
            held(18, ROWS, 128),
            held(36, ROWS, 128),
            held(36, ROWS, 128),
            held(36, ROWS, 128),
            held(18, ROWS, 128),
            FORCE,
        ),
        in_specs=[HBM] + [VM] * 8,
        out_specs=[VM] * 5 + [HBM],
        input_output_aliases={4: 0, 5: 1, 6: 2, 7: 3, 8: 4},
        scratch_shapes=[dma((9,)), dma((12,))],
    )(links, uz, xs, ys, ux, *work)
    fx, force = kernel_call(
        edge_back_kernel,
        "edge_back",
        EDGE_BACK_COST,
        out_shape=(held(18, ROWS, 128), FORCE),
        in_specs=[VM] * 5 + [HBM],
        out_specs=[VM, HBM],
        input_output_aliases={4: 0, 5: 1},
        scratch_shapes=[held(12, YB * 8, 128)],
    )(xb, ux, ys, pre, fx, force)
    fz, force = kernel_call(
        edge_z_kernel,
        "edge_z",
        EDGE_Z_COST,
        out_shape=(held(18, ROWS, 128), FORCE),
        in_specs=[VM] * 7 + [HBM],
        out_specs=[VM, HBM],
        input_output_aliases={7: 1},
        scratch_shapes=[held(24, ROWS, 128), dma((4,))],
    )(far, near, uz, xs, ys, pre, fs, force)
    return kernel_call(
        edge_ahead_kernel,
        "edge_ahead",
        4000000,
        out_shape=FORCE,
        in_specs=[VM] * 7 + [HBM],
        out_specs=HBM,
        input_output_aliases={7: 0},
        scratch_shapes=[held(18, ROWS, 128), held(18, YB * 8, 128), dma((8,))],
    )(xf, ux, xs, ys, pre, fx, fz, force)


def solution(mesh):
    placed = (P(None, None, "xy", "zt", None), P(None, "xy", "zt", None), P(None, "xy", "zt", None))
    return jax.shard_map(
        per_device,
        mesh=mesh,
        in_specs=placed,
        out_specs=P(None, None, "xy", "zt", None),
        check_vma=False,
    )
```

```python
import jax
import jax.numpy as jnp
from jax import lax
from jax.experimental import pallas as pl
from jax.experimental.pallas import tpu as pltpu
from jax.sharding import PartitionSpec as P

NT = 24
CX, CZ, YT, YB = 8, 4, 384, 3
ROWS = YB * CX * CZ

coef_one = 9.0 / 8.0
coef_naik = -1.0 / 24.0

F32 = jnp.float32

LOCAL_COST = 1000000
EDGE_Z_COST = 4000000
EDGE_BACK_COST = 2000000000

AHEAD = (2, 0)


def mat_vec(u, v):
    out_r, out_i = [], []
    for a in range(3):
        re = im = None
        for b in range(3):
            ur, ui = u(3 * a + b), u(9 + 3 * a + b)
            r = ur * v[b] - ui * v[3 + b]
            i = ur * v[3 + b] + ui * v[b]
            re, im = (r, i) if re is None else (re + r, im + i)
        out_r.append(re)
        out_i.append(im)
    return out_r + out_i


def adj_vec(u, v):
    out_r, out_i = [], []
    for a in range(3):
        re = im = None
        for b in range(3):
            ur, ui = u(3 * b + a), u(9 + 3 * b + a)
            r = ur * v[b] + ui * v[3 + b]
            i = ur * v[3 + b] - ui * v[b]
            re, im = (r, i) if re is None else (re + r, im + i)
        out_r.append(re)
        out_i.append(im)
    return out_r + out_i


def store_force(put, v1, y, p1, q1, x, q2):
    for a in range(3):
        for b in range(3):
            re = im = None
            for p, q in ((v1, y), (p1, q1), (x, q2)):
                r = p[a] * q[b] + p[3 + a] * q[3 + b]
                i = p[3 + a] * q[b] - p[a] * q[3 + b]
                re, im = (r, i) if re is None else (re + r, im + i)
            put(3 * a + b, re)
            put(9 + 3 * a + b, im)


def tiles(ref):
    return ref.reshape(ref.shape[0], YB, CX, CZ, 128)


def lanes(yb):
    return pl.ds(128 * yb, 128)


class Loads:
    def __init__(self, sem):
        self.sem, self.copies, self.count = sem, {}, 0

    def start(self, name, src, dst):
        copy = pltpu.make_async_copy(src, dst, self.sem.at[self.count])
        copy.start()
        self.copies.setdefault(name, []).append(copy)
        self.count += 1

    def wait(self, name):
        for copy in self.copies.pop(name):
            copy.wait()


def vector(ref, rows, first=0):
    return [ref[first + c, rows, :] for c in range(6)]


def prep_kernel(links, sol, prod, far, near, xf, xb, ux, uz, xs, ys, sem):
    loads = Loads(sem)
    uxt, uzt, xst, yst = tiles(ux), tiles(uz), tiles(xs), tiles(ys)
    for yb in range(YB):
        loads.start("x", sol.at[:, :, :, lanes(yb)], xst.at[:, yb])
    for yb in range(YB):
        loads.start("uz", links.at[2, :, :, :, lanes(yb)], uzt.at[:, yb])
    for yb in range(YB):
        loads.start("y", prod.at[:, :, :, lanes(yb)], yst.at[:, yb])
    for first in (0, CX - 2):
        for yb in range(YB):
            src = links.at[0, :, pl.ds(first, 2), :, lanes(yb)]
            loads.start("ux", src, uxt.at[:, yb, pl.ds(first, 2)])

    def layer(z):
        return pl.ds(z, YB * CX, stride=CZ)

    def u_z(z):
        return lambda c: uz[c, layer(z), :]

    loads.wait("x")
    loads.wait("uz")
    p1 = mat_vec(u_z(0), vector(xs, layer(1)))
    p2 = mat_vec(u_z(0), mat_vec(u_z(1), vector(xs, layer(2))))
    ahead = vector(xs, layer(0)) + p1 + p2
    loads.wait("y")
    q1 = [coef_naik * v for v in adj_vec(u_z(3), vector(ys, layer(3)))]
    q2 = adj_vec(u_z(3), [coef_naik * v for v in adj_vec(u_z(2), vector(ys, layer(2)))])
    behind = q1 + q2

    def put(to_before, to_after):
        for c, value in enumerate(ahead):
            to_before[c] = value
        for c, value in enumerate(behind):
            to_after[c] = value

    odd = lax.axis_index("zt") % 2
    pl.when(odd == 0)(lambda: put(far, near))
    pl.when(odd == 1)(lambda: put(near, far))
    loads.wait("ux")

    def u_x(row):
        return lambda c: ux[c, pl.ds(row, 8), :]

    for yb in range(YB):
        last = yb * CX * CZ + (CX - 2) * CZ
        w1 = [coef_naik * v for v in adj_vec(u_x(last), vector(ys, pl.ds(last, 8)))]
        w2 = adj_vec(u_x(last), [pltpu.roll(v, 4, 0) for v in w1])
        for c, value in enumerate(w1 + w2):
            xb[c, yb] = value[CZ:]
        base = yb * CX * CZ
        p1 = mat_vec(u_x(base), vector(xs, pl.ds(base + CZ, 8)))
        p2 = mat_vec(u_x(base), [pltpu.roll(v, 4, 0) for v in p1])
        for c, value in enumerate(vector(xs, pl.ds(base, 8)) + p1 + p2):
            xf[c, yb] = value[:CZ]


def move_y(v, step):
    lane = lax.broadcasted_iota(jnp.int32, (8, 128), 1)
    if step > 0:
        r = [pltpu.roll(a, 128 - NT, 1) for a in v]
        return [jnp.where(lane < 128 - NT, r[k], r[(k + 1) % YB]) for k in range(YB)]
    r = [pltpu.roll(a, NT, 1) for a in v]
    return [jnp.where(lane >= NT, r[k], r[(k - 1) % YB]) for k in range(YB)]


def move_t(v, step):
    lane = lax.broadcasted_iota(jnp.int32, (8, 128), 1)
    out = []
    if step > 0:
        near = [pltpu.roll(a, 127, 1) for a in v]
        wrap = [pltpu.roll(a, NT - 1, 1) for a in v]
        for k in range(YB):
            edge = (lane + 128 * k) % NT == NT - 1
            far = wrap[k] if k == 0 else jnp.where(lane < NT - 1, wrap[k - 1], wrap[k])
            beside = near[k] if k == YB - 1 else jnp.where(lane == 127, near[k + 1], near[k])
            out.append(jnp.where(edge, far, beside))
        return out
    near = [pltpu.roll(a, 1, 1) for a in v]
    wrap = [pltpu.roll(a, 128 - (NT - 1), 1) for a in v]
    for k in range(YB):
        edge = (lane + 128 * k) % NT == 0
        far = wrap[k] if k == YB - 1 else jnp.where(lane >= 128 - (NT - 1), wrap[k + 1], wrap[k])
        beside = near[k] if k == 0 else jnp.where(lane == 0, near[k - 1], near[k])
        out.append(jnp.where(edge, far, beside))
    return out


def local_piece(d, piece, move, ul, xs, ys, fs):
    rows = [pl.ds(pl.multiple_of(yb * CX * CZ + piece * 8, 8), 8) for yb in range(YB)]

    def shift(vecs, step):
        moved = [move([vecs[k][c] for k in range(YB)], step) for c in range(6)]
        return [[moved[c][k] for c in range(6)] for k in range(YB)]

    def u(k):
        return lambda c: ul[18 * d + c, rows[k], :]

    x = shift([vector(xs, r) for r in rows], 1)
    p1 = shift([mat_vec(u(k), x[k]) for k in range(YB)], 1)
    p2 = shift([mat_vec(u(k), p1[k]) for k in range(YB)], 1)
    v1 = [[coef_one * a + coef_naik * b for a, b in zip(x[k], p2[k])] for k in range(YB)]
    y = [vector(ys, r) for r in rows]
    q1 = [adj_vec(u(k), y[k]) for k in range(YB)]
    q1 = shift([[coef_naik * a for a in v] for v in q1], -1)
    q2 = shift([adj_vec(u(k), q1[k]) for k in range(YB)], -1)
    for k in range(YB):

        def put(c, value, k=k):
            fs[18 * d + c, rows[k], :] = value

        store_force(put, v1[k], y[k], p1[k], q1[k], x[k], q2[k])


def load_local(loads, links, ux, ul):
    for yb in range(YB):
        src = links.at[0, :, pl.ds(2, CX - 4), :, lanes(yb)]
        loads.start(0, src, tiles(ux).at[:, yb, pl.ds(2, CX - 4)])
    for d, mu in enumerate((1, 3)):
        for yb in range(YB):
            src, dst = links.at[mu, :, :, :, lanes(yb)], tiles(ul).at[pl.ds(18 * d, 18), yb]
            loads.start(mu, src, dst)


def local_pieces(d, first, end, ul, xs, ys, fs, sent=None):
    def body(piece, carry):
        local_piece(d, piece, (move_y, move_t)[d], ul, xs, ys, fs)
        if sent is not None:
            sent(piece)
        return carry

    lax.fori_loop(first, end, body, 0)


def slices(yb):
    return [pl.ds(pl.multiple_of(yb * CX * CZ + k * 8, 8), 8) for k in range(4)]


def halves(vec):
    return [pltpu.roll(a, CZ, 0) for a in vec]


def joined(first, second):
    low = lax.broadcasted_iota(jnp.int32, (8, 128), 0) < CZ
    return [jnp.where(low, a, b) for a, b in zip(first, second)]


def scaled(vec):
    return [coef_naik * a for a in vec]


def mixed(x, p2):
    return [coef_one * a + coef_naik * b for a, b in zip(x, p2)]


def first_products(loads, ux, uz, xs, ys, pre, fx):
    def body_z(piece, carry):
        rows = pl.ds(pl.multiple_of(piece * 8, 8), 8)
        p1 = mat_vec(lambda c: uz[c, rows, :], [pltpu.roll(a, 7, 0) for a in vector(xs, rows)])
        w1 = scaled(adj_vec(lambda c: uz[c, rows, :], vector(ys, rows)))
        for c, value in enumerate(p1 + w1):
            pre[c, rows, :] = value
        return carry

    lax.fori_loop(0, ROWS // 8, body_z, 0)
    loads.wait(0)

    def body_x(yb, carry):
        rows = slices(yb)

        def u(k):
            return lambda c: ux[c, rows[k], :]

        def keep(k, vecs):
            for c, value in enumerate(sum(vecs, [])):
                pre[12 + c, rows[k], :] = value

        y = [vector(ys, r) for r in rows]
        h = [halves(vector(xs, r)) for r in rows]
        x = [joined(h[k], h[k + 1]) for k in range(3)]
        p1_raw = [mat_vec(u(k), x[k]) for k in range(3)]
        h = [halves(v) for v in p1_raw]
        p1 = [joined(h[0], h[1]), joined(h[1], h[2]), h[2]]
        h = [halves(mat_vec(u(k), p1[k])) for k in range(3)]
        v1 = [mixed(x[k], joined(h[k], h[k + 1])) for k in range(2)]
        w1 = [scaled(adj_vec(u(k), y[k])) for k in range(4)]
        h = [halves(v) for v in w1]
        q1 = [h[0]] + [joined(h[k - 1], h[k]) for k in (1, 2, 3)]
        h = [halves(adj_vec(u(k), q1[k])) for k in range(4)]
        q2 = [None] + [joined(h[k - 1], h[k]) for k in (1, 2, 3)]
        keep(0, [v1[0], p1[0], x[0], w1[0]])
        keep(2, [q1[2], q2[2], p1_raw[2]])
        keep(3, [q1[3], q2[3]])

        def put(c, value):
            fx[c, rows[1], :] = value

        store_force(put, v1[1], y[1], p1[1], q1[1], x[1], q2[1])
        return carry

    lax.fori_loop(0, YB, body_x, 0)


def early_kernel(links, uz, xs, ys, _, __, far, ux, ul, fs, pre, fx, sem):
    @pl.when(lax.axis_index("zt") == 0)
    def _():
        loads = Loads(sem)
        load_local(loads, links, ux, ul)
        first_products(loads, ux, uz, xs, ys, pre, fx)
        for d, mu in enumerate((1, 3)):
            loads.wait(mu)
            local_pieces(d, 0, AHEAD[d], ul, xs, ys, fs)


def local_kernel(links, uz, xs, ys, *refs):
    ux, ul, fs, pre, fx, force, sem, sem_out = refs[5:]
    first = lax.axis_index("zt") == 0
    fst = tiles(fs)

    def out_copy(piece, yb):
        return pltpu.make_async_copy(
            fst.at[pl.ds(0, 18), yb, pl.ds(2 * piece, 2)],
            force.at[1, :, pl.ds(2 * piece, 2), :, lanes(yb)],
            sem_out.at[yb * 4 + piece],
        )

    def sent(piece):
        for yb in range(YB):
            out_copy(piece, yb).start()

    @pl.when(first)
    def _():
        for piece in range(AHEAD[0]):
            sent(piece)
        local_pieces(0, AHEAD[0], 4, ul, xs, ys, fs, sent)
        local_pieces(1, AHEAD[1], 4, ul, xs, ys, fs)

    @pl.when(jnp.logical_not(first))
    def _():
        loads = Loads(sem)
        load_local(loads, links, ux, ul)
        first_products(loads, ux, uz, xs, ys, pre, fx)
        loads.wait(1)
        local_pieces(0, 0, 4, ul, xs, ys, fs, sent)
        loads.wait(3)
        local_pieces(1, 0, 4, ul, xs, ys, fs)

    for yb in range(YB):
        for piece in range(4):
            out_copy(piece, yb).wait()


def edge_back_kernel(xb, ux, ys, pre, _, __, fx, force, hx):
    for yb in range(YB):
        for c in range(12):
            hx[c, pl.ds(yb * 8, CZ), :] = xb[c, yb]
    for yb in range(YB):
        rows = slices(yb)[0]
        edge = pl.ds(yb * 8, 8)
        q1 = joined(vector(hx, edge), halves(vector(pre, rows, 30)))
        w2 = adj_vec(lambda c: ux[c, rows, :], q1)
        q2 = joined(vector(hx, edge, 6), halves(w2))

        def put(c, value):
            fx[c, rows, :] = value

        v1, p1, x = (vector(pre, rows, first) for first in (12, 18, 24))
        store_force(put, v1, vector(ys, rows), p1, q1, x, q2)


def edge_ahead_kernel(xf, ux, xs, ys, pre, fx, fz, _, force, f2, hx, sem):
    for yb in range(1, YB):
        out_z(fz, force, yb, sem.at[2 * YB + yb - 1]).start()

    def out_copy(src, first, yb):
        return pltpu.make_async_copy(
            tiles(src).at[:, yb, pl.ds(first, CX // 2)],
            force.at[0, :, pl.ds(first, CX // 2), :, lanes(yb)],
            sem.at[first // 4 * YB + yb],
        )

    for yb in range(YB):
        out_copy(fx, 0, yb).start()
        for c in range(18):
            hx[c, pl.ds(yb * 8 + CZ, CZ), :] = xf[c, yb]
    for yb in range(YB):
        rows = slices(yb)
        edge = pl.ds(yb * 8, 8)

        def u(k):
            return lambda c: ux[c, rows[k], :]

        def ahead(second, third, first):
            h = [halves(second), halves(third), vector(hx, edge, first)]
            return {2: joined(h[0], h[1]), 3: joined(h[1], h[2])}

        x = ahead(vector(xs, rows[2]), vector(xs, rows[3]), 0)
        p1 = ahead(vector(pre, rows[2], 24), mat_vec(u(3), x[3]), 6)
        p2 = ahead(mat_vec(u(2), p1[2]), mat_vec(u(3), p1[3]), 12)
        for k in (2, 3):

            def put(c, value, k=k):
                f2[c, rows[k], :] = value

            q1, q2 = vector(pre, rows[k], 12), vector(pre, rows[k], 18)
            store_force(put, mixed(x[k], p2[k]), vector(ys, rows[k]), p1[k], q1, x[k], q2)
        out_copy(f2, CX // 2, yb).start()
    for first, src in ((0, fx), (CX // 2, f2)):
        for yb in range(YB):
            out_copy(src, first, yb).wait()
    for yb in range(1, YB):
        out_z(fz, force, yb, sem.at[2 * YB + yb - 1]).wait()


def out_z(fz, force, yb, sem):
    return pltpu.make_async_copy(tiles(fz).at[:, yb], force.at[2, :, :, :, lanes(yb)], sem)


def edge_z_kernel(far, near, ul, xs, ys, pre, fs, _, fz, force, hz, sem):
    def out_t(yb):
        return pltpu.make_async_copy(
            tiles(fs).at[pl.ds(18, 18), yb], force.at[3, :, :, :, lanes(yb)], sem.at[yb]
        )

    for yb in range(YB):
        out_t(yb).start()
    top_rows = pl.ds(CZ - 1, YB * CX, stride=CZ)

    def spread(zf, zb):
        p1 = mat_vec(lambda c: ul[c, top_rows, :], [zf[c] for c in range(6)])
        for c, value in enumerate([zf[c] for c in range(18)] + p1):
            hz[c, top_rows, :] = value
        for c in range(12):
            hz[c, pl.ds(0, YB * CX, stride=CZ), :] = zb[c]

    odd = lax.axis_index("zt") % 2
    pl.when(odd == 0)(lambda: spread(near, far))
    pl.when(odd == 1)(lambda: spread(far, near))
    row = lax.broadcasted_iota(jnp.int32, (8, 128), 0)
    top, bottom = row % CZ == CZ - 1, row % CZ == 0

    def body(piece, yb):
        rows = pl.ds(pl.multiple_of(yb * CX * CZ + piece * 8, 8), 8)

        def ahead(v, first):
            halo = vector(hz, rows, first)
            return [jnp.where(top, h, pltpu.roll(a, 7, 0)) for a, h in zip(v, halo)]

        def back(v, first):
            halo = vector(hz, rows, first)
            return [jnp.where(bottom, h, pltpu.roll(a, 1, 0)) for a, h in zip(v, halo)]

        def u(c):
            return ul[c, rows, :]

        x = ahead(vector(xs, rows), 0)
        own = [jnp.where(top, h, a) for a, h in zip(vector(pre, rows), vector(hz, rows, 18))]
        p1 = ahead(own, 6)
        p2 = ahead(mat_vec(u, p1), 12)
        v1 = [coef_one * a + coef_naik * b for a, b in zip(x, p2)]
        y = vector(ys, rows)
        q1 = back(vector(pre, rows, 6), 0)
        q2 = back(adj_vec(u, q1), 6)

        def put(c, value):
            fz[c, rows, :] = value

        store_force(put, v1, y, p1, q1, x, q2)
        return yb

    for yb in range(YB):
        lax.fori_loop(0, 4, body, yb)
        if yb == 0:
            out_z(fz, force, yb, sem.at[YB]).start()
    for yb in range(YB):
        out_t(yb).wait()
    out_z(fz, force, 0, sem.at[YB]).wait()


HBM = pl.BlockSpec(memory_space=pltpu.HBM)
VM = pl.BlockSpec(memory_space=pltpu.VMEM)
FORCE = jax.ShapeDtypeStruct((4, 18, CX, CZ, YT), F32)


def held(*shape):
    return pltpu.VMEM(shape, F32)


def kernel_call(body, name, flops, **args):
    return pl.pallas_call(
        body,
        name=name,
        cost_estimate=pl.CostEstimate(flops=flops, bytes_accessed=flops, transcendentals=0),
        compiler_params=pltpu.CompilerParams(vmem_limit_bytes=16 << 20),
        **args,
    )


def shifted(value, axis, step):
    size = lax.axis_size(axis)
    return lax.ppermute(value, axis, [(i, (i + step) % size) for i in range(size)])


def per_device(links, solution, product):
    links, solution, product = (
        pltpu.with_memory_space_constraint(a, pltpu.HBM) for a in (links, solution, product)
    )
    dma = pltpu.SemaphoreType.DMA
    far, near, xf, xb, ux, uz, xs, ys = kernel_call(
        prep_kernel,
        "prep",
        3000000,
        out_shape=(
            held(18, YB * CX, 128),
            held(28, YB * CX, 128),
            held(18, YB, CZ, 128),
            held(12, YB, CZ, 128),
            held(18, ROWS, 128),
            held(18, ROWS, 128),
            held(6, ROWS, 128),
            held(6, ROWS, 128),
        ),
        in_specs=[HBM] * 3,
        out_specs=[VM] * 8,
        scratch_shapes=[dma((15,))],
    )(links, solution, product)
    size = lax.axis_size("zt")
    near = lax.ppermute(near, "zt", [(i, i ^ 1) for i in range(size)])
    far, ux, *work = kernel_call(
        early_kernel,
        "early",
        1000000,
        out_shape=(
            held(18, YB * CX, 128),
            held(18, ROWS, 128),
            held(36, ROWS, 128),
            held(36, ROWS, 128),
            held(36, ROWS, 128),
            held(18, ROWS, 128),
        ),
        in_specs=[HBM] + [VM] * 5,
        out_specs=[VM] * 6,
        input_output_aliases={4: 0, 5: 1},
        scratch_shapes=[dma((9,))],
    )(links, uz, xs, ys, far, ux)
    far = lax.ppermute(far, "zt", [(i, (i + 2 * (i % 2) - 1) % size) for i in range(size)])
    xb = shifted(xb, "xy", 1)
    xf = shifted(xf, "xy", -1)
    ux, _, fs, pre, fx, force = kernel_call(
        local_kernel,
        "local",
        LOCAL_COST,
        out_shape=(
            held(18, ROWS, 128),
            held(36, ROWS, 128),
            held(36, ROWS, 128),
            held(36, ROWS, 128),
            held(18, ROWS, 128),
            FORCE,
        ),
        in_specs=[HBM] + [VM] * 8,
        out_specs=[VM] * 5 + [HBM],
        input_output_aliases={4: 0, 5: 1, 6: 2, 7: 3, 8: 4},
        scratch_shapes=[dma((9,)), dma((12,))],
    )(links, uz, xs, ys, ux, *work)
    fx, force = kernel_call(
        edge_back_kernel,
        "edge_back",
        EDGE_BACK_COST,
        out_shape=(held(18, ROWS, 128), FORCE),
        in_specs=[VM] * 5 + [HBM],
        out_specs=[VM, HBM],
        input_output_aliases={4: 0, 5: 1},
        scratch_shapes=[held(12, YB * 8, 128)],
    )(xb, ux, ys, pre, fx, force)
    fz, force = kernel_call(
        edge_z_kernel,
        "edge_z",
        EDGE_Z_COST,
        out_shape=(held(18, ROWS, 128), FORCE),
        in_specs=[VM] * 7 + [HBM],
        out_specs=[VM, HBM],
        input_output_aliases={7: 1},
        scratch_shapes=[held(24, ROWS, 128), dma((4,))],
    )(far, near, uz, xs, ys, pre, fs, force)
    return kernel_call(
        edge_ahead_kernel,
        "edge_ahead",
        4000000,
        out_shape=FORCE,
        in_specs=[VM] * 7 + [HBM],
        out_specs=HBM,
        input_output_aliases={7: 0},
        scratch_shapes=[held(18, ROWS, 128), held(18, YB * 8, 128), dma((8,))],
    )(xf, ux, xs, ys, pre, fx, fz, force)


def solution(mesh):
    placed = (P(None, None, "xy", "zt", None), P(None, "xy", "zt", None), P(None, "xy", "zt", None))
    return jax.shard_map(
        per_device,
        mesh=mesh,
        in_specs=placed,
        out_specs=P(None, None, "xy", "zt", None),
        check_vma=False,
    )
```
